512 devices in a mesh: video: 16 (over y, z_hi), audio: 8 (over x, core), tp: 4 (over z_lo).
Axes of the slice: x: 4, y: 4, z: 16 (z_hi: 4, z_lo: 4; z = z_hi * 4 + z_lo), core: 2. Of those that a mesh axis runs over, the one named last changes fastest.
Arguments:
- video_query: bfloat16 [81920, 3072], P(('video', 'audio'), 'tp')
- audio_key: bfloat16 [16384, 3072], P(('video', 'audio'), 'tp')
- audio_value: bfloat16 [16384, 3072], P(('video', 'audio'), 'tp'), may hold values from -6 to 6
- cotangent: bfloat16 [81920, 3072], P(('video', 'audio'), 'tp')
- query_gain: float32 [3072], P('tp'), may hold values from 0.5 to 2
- key_gain: float32 [3072], P('tp'), may hold values from 0.5 to 2
- time_lists: int32 [640, 4], P(('video', 'audio')), may hold values from 0 to 127, as said below
Outputs:
- attended: bfloat16 [81920, 3072], P(('video', 'audio'), 'tp')
- video_query_grad: bfloat16 [81920, 3072], P(('video', 'audio'), 'tp')
- audio_key_grad: bfloat16 [16384, 3072], P(('video', 'audio'), 'tp')
- audio_value_grad: bfloat16 [16384, 3072], P(('video', 'audio'), 'tp')
- query_gain_grad: float32 [3072], P('tp')
- key_gain_grad: float32 [3072], P('tp')
The draws below stay inside these ranges and needn't reach their ends.
Inputs may be any that keep to these rules, and one draw needn't show every extreme that they name: `time_lists`: row b lists audio blocks for video block b. Its first entry is (b) // 5; every entry differs from that value by at most 1, and in every row one entry lies exactly 1 below or above it before clipping to the range.
All inputs are finite; a program needn't handle non-finite values.
Results may differ from the reference program's by a relative error of at most 0.015.
The reference program's roundings to bfloat16 on the way (of `query_norm`, `key_norm`, `probs_low` and `grad_scores`) count: a program that leaves them out, or rounds other values in their place, can miss the bound.
Values may be sent and summed in bfloat16 or wider, within the bound.
No kernel may reach another device: no remote copies, remote signals or barrier semaphores. Data moves between devices by JAX's collectives and lax.ppermute only.
A program may use at most 64 MiB of HBM per device.

```python
import math
import jax
import jax.numpy as jnp
from jax import lax

D = 3072
H = 24
HS = 128
BLOCK = 128
VT_DEV = 640
AT_DEV = 128
VB_DEV = 5
AB_DEV = 1
NV = 81920
NA = 16384
NVB = 640
NAB = 128
N_VIDEO = 16
N_AUDIO = 8


def audio_keys(key, boost, spread):
    noise = jax.random.normal(jax.random.fold_in(key, 11), (NA, D), jnp.float32)
    position = jnp.arange(NA, dtype=jnp.int32) % BLOCK
    head_of = (jnp.arange(D, dtype=jnp.int32) // HS)[None, :]
    target = (jnp.arange(NA, dtype=jnp.int32) // BLOCK % H)[:, None]
    focus = jnp.logical_and(jnp.logical_or(position == 7, position == 8)[:, None], head_of == target)
    noise = noise * (1.0 + boost * focus.astype(jnp.float32))
    rows = jnp.exp(jax.random.uniform(jax.random.fold_in(key, 12), (NA, 1), jnp.float32) * math.log(spread))
    columns = jnp.exp(jnp.arange(D, dtype=jnp.float32) / D * math.log(3.0))[None, :]
    return noise * rows * columns


def draw_audio_key(key, part):
    result = audio_keys(key, 0.0, 10.0)
    return result.astype(jnp.bfloat16)


def draw_video_query(key, part):
    spread = 10.0
    key = jax.random.fold_in(key, 4)
    noise = jax.random.normal(jax.random.fold_in(key, 1), (NV, D), jnp.float32)
    rows = jnp.exp(jax.random.uniform(jax.random.fold_in(key, 2), (NV, 1), jnp.float32) * math.log(spread))
    columns = jnp.exp(jnp.arange(D, dtype=jnp.float32) / D * math.log(3.0))[None, :]
    result = noise * rows * columns
    return result.astype(jnp.bfloat16)


def draw_cotangent(key, part):
    key = jax.random.fold_in(key, 5)
    rising = (1.0 + 2.0 * jnp.arange(NV, dtype=jnp.float32) / NV)[:, None]
    noise = jax.random.normal(jax.random.fold_in(key, 1), (NV, D), jnp.float32)
    return (jnp.clip(noise, -6.0, 6.0) * rising).astype(jnp.bfloat16)


def draw_time_lists(key, part):
    key = jax.random.fold_in(key, 6)
    blocks = jnp.arange(NVB, dtype=jnp.int32)
    center = blocks * AB_DEV // VB_DEV
    side = jax.random.randint(jax.random.fold_in(key, 1), (NVB,), 0, 2, dtype=jnp.int32)
    side = jnp.where(blocks == NVB - 1, 1, side)
    first = center + (2 * side - 1) * AB_DEV
    others = center[:, None] + jax.random.randint(jax.random.fold_in(key, 2), (NVB, 2), -AB_DEV, AB_DEV + 1, dtype=jnp.int32)
    listed = jnp.concatenate([center[:, None], first[:, None], others], axis=1)
    return jnp.clip(listed, 0, NAB - 1).astype(jnp.int32)


def steps_of(key, extent, shards, smallest, top_value):
    def one(axis_at, parts):
        heights = jax.random.uniform(jax.random.fold_in(jax.random.fold_in(key, 6), axis_at), (parts,), jnp.float32, smallest / len(shards), top_value / len(shards))
        return jnp.repeat(jnp.exp(heights), extent[axis_at] // parts).reshape((-1,) + (1,) * (len(extent) - axis_at - 1))

    level = one(*shards[0])
    for cut in shards[1:]:
        level = level * one(*cut)
    return level


def centred(rng, shape, width, limit, cuts=(), kind=jnp.bfloat16):
    level = steps_of(rng, shape, cuts, -0.22, 0.18) if cuts else 1.0
    entries = jax.random.normal(rng, shape, jnp.float32) * width * level
    return jnp.minimum(jnp.maximum(entries, -limit), limit).astype(kind)


def setup_inputs(seed: int = 0) -> dict:
    arg_keys = jax.random.split(jax.random.key(seed), 8)
    video_query = draw_video_query(jax.random.fold_in(arg_keys[7], 71), 0)
    audio_key = draw_audio_key(jax.random.fold_in(arg_keys[7], 71), 0)
    audio_value = centred(arg_keys[2], (NA, D), 1.0, 6.0, ((0, 128), (1, 4)))
    cotangent = draw_cotangent(jax.random.fold_in(arg_keys[7], 71), 0)
    query_gain = jnp.clip(jnp.exp(math.log(2.0) - 1.3862944 * jax.random.uniform(arg_keys[4], (D,), jnp.float32) ** steps_of(arg_keys[4], (D,), ((0, 4),), -0.2, 0.2)), 0.5, 2.0)
    key_gain = jnp.clip(jnp.exp(math.log(2.0) - 1.3862944 * jax.random.uniform(arg_keys[5], (D,), jnp.float32) ** steps_of(arg_keys[5], (D,), ((0, 4),), -0.2, 0.2)), 0.5, 2.0)
    time_lists = draw_time_lists(jax.random.fold_in(arg_keys[7], 71), 0)
    return dict(video_query=video_query, audio_key=audio_key, audio_value=audio_value, cotangent=cotangent, query_gain=query_gain, key_gain=key_gain, time_lists=time_lists)


epsilon = 1e-06
excluded = -1e+30

def inverse_rms(rows):
    return lax.rsqrt(lax.optimization_barrier(jnp.mean(rows * rows, axis=1)) + epsilon)

def rounded(values):
    return lax.optimization_barrier(values.astype(jnp.bfloat16)).astype(jnp.float32)

def token_mask(allowed):
    count_rows, count_cols = allowed.shape
    spread = jnp.broadcast_to(allowed[:, None, :, None], (count_rows, BLOCK, count_cols, BLOCK))
    return spread.reshape(count_rows * BLOCK, count_cols * BLOCK)

def norm_backward(rows, scale, gain, upstream):
    scaled = upstream * gain
    inner = lax.optimization_barrier(jnp.sum(rows * scaled, axis=1))
    grad_rows = scale[:, None] * scaled - rows * (scale * scale * scale * inner / D)[:, None]
    grad_gain = lax.optimization_barrier(jnp.sum(upstream * rows * scale[:, None], axis=0))
    return (grad_rows.astype(jnp.bfloat16), grad_gain)

def reference(video_query, audio_key, audio_value, cotangent, query_gain, key_gain, time_lists):
    factor = HS ** (-0.5)
    query_rows = video_query.astype(jnp.float32)
    key_rows = audio_key.astype(jnp.float32)
    query_scale = inverse_rms(query_rows)
    key_scale = inverse_rms(key_rows)
    query_norm = (query_rows * query_scale[:, None] * query_gain).astype(jnp.bfloat16)
    key_norm = (key_rows * key_scale[:, None] * key_gain).astype(jnp.bfloat16)
    padding = jnp.zeros((AT_DEV, D), jnp.bfloat16)
    key_padded = jnp.concatenate([padding, key_norm, padding], axis=0)
    value_padded = jnp.concatenate([padding, audio_value, padding], axis=0)
    window = 3 * AT_DEV

    def one_group(carry, group):
        key_total, value_total = carry
        queries = lax.dynamic_slice_in_dim(query_norm, group * VT_DEV, VT_DEV, 0).astype(jnp.float32).reshape(VT_DEV, H, HS)
        upstream = lax.dynamic_slice_in_dim(cotangent, group * VT_DEV, VT_DEV, 0).astype(jnp.float32).reshape(VT_DEV, H, HS)
        lists = lax.dynamic_slice_in_dim(time_lists, group * VB_DEV, VB_DEV, 0)
        keys = lax.dynamic_slice_in_dim(key_padded, group * AT_DEV, window, 0).astype(jnp.float32).reshape(window, H, HS)
        values = lax.dynamic_slice_in_dim(value_padded, group * AT_DEV, window, 0).astype(jnp.float32).reshape(window, H, HS)
        block_ids = (group - 1) * AB_DEV + jnp.arange(3 * AB_DEV, dtype=jnp.int32)
        allowed = jnp.any(lists[:, :, None] == block_ids[None, None, :], axis=1)
        mask = token_mask(allowed)
        scores = jnp.einsum('qhd,khd->hqk', queries, keys) * factor
        scores = jnp.where(mask[None], scores, excluded)
        highest = lax.optimization_barrier(jnp.max(scores, axis=2, keepdims=True))
        log_total = highest + jnp.log(lax.optimization_barrier(jnp.sum(jnp.exp(scores - highest), axis=2, keepdims=True)))
        probs = jnp.exp(scores - log_total)
        probs_low = rounded(probs)
        output = rounded(jnp.einsum('hqk,khd->qhd', probs_low, values))
        row_delta = lax.optimization_barrier(jnp.sum(upstream * output, axis=2))
        grad_probs = jnp.einsum('qhd,khd->hqk', upstream, values)
        grad_scores = rounded(probs * (grad_probs - row_delta.T[:, :, None]) * factor)
        grad_query = jnp.einsum('hqk,khd->qhd', grad_scores, keys).reshape(VT_DEV, D)
        grad_keys = jnp.einsum('hqk,qhd->khd', grad_scores, queries).reshape(window, D)
        grad_values = jnp.einsum('hqk,qhd->khd', probs_low, upstream).reshape(window, D)
        start = group * AT_DEV
        key_total = lax.dynamic_update_slice_in_dim(key_total, lax.dynamic_slice_in_dim(key_total, start, window, 0) + grad_keys, start, 0)
        value_total = lax.dynamic_update_slice_in_dim(value_total, lax.dynamic_slice_in_dim(value_total, start, window, 0) + grad_values, start, 0)
        return ((key_total, value_total), (output.reshape(VT_DEV, D).astype(jnp.bfloat16), grad_query))
    groups = N_VIDEO * N_AUDIO
    zeros = jnp.zeros((NA + 2 * AT_DEV, D), jnp.float32)
    (key_total, value_total), (attended, grad_query) = lax.scan(one_group, (zeros, zeros), jnp.arange(groups, dtype=jnp.int32))
    attended = attended.reshape(NV, D)
    grad_query = grad_query.reshape(NV, D)
    grad_key = key_total[AT_DEV:AT_DEV + NA]
    audio_value_grad = value_total[AT_DEV:AT_DEV + NA].astype(jnp.bfloat16)
    video_query_grad, query_gain_grad = norm_backward(query_rows, query_scale, query_gain, grad_query)
    audio_key_grad, key_gain_grad = norm_backward(key_rows, key_scale, key_gain, grad_key)
    return (attended, video_query_grad, audio_key_grad, audio_value_grad, query_gain_grad, key_gain_grad)
```

```python
import functools
import numpy as np
import jax
import jax.numpy as jnp
from jax import lax
from jax.experimental import pallas as pl
from jax.experimental.pallas import tpu as pltpu
from jax.sharding import Mesh, PartitionSpec as P

D = 3072
HS = 128
BLOCK = 128
FACTOR = HS ** (-0.5)
LOG2E = 1.4426950408889634
EPSILON = 1e-06
EXCLUDED = -1e30
LINE = ("y", "far", "x", "core")


def by_last(left, right):
    return lax.dot_general(
        left, right, (((1,), (1,)), ((), ())), preferred_element_type=jnp.float32
    )


def plain(left, right):
    return jnp.dot(left, right, preferred_element_type=jnp.float32)


def attention_kernel(
    bias, scale, query, cot, gain, key_gain, key_l, key_c, key_r, val_l, val_c, val_r,
    attended, grad_query, inner, query_gain_grad, key_gain_grad, left, right, own,
    scale_cols, inner_sum, probs_low, grad_low,
):
    head = pl.program_id(0)
    rows = query.shape[0]

    @pl.when(head == 0)
    def _():
        scale_cols[...] = jnp.broadcast_to(scale[...], (HS, rows)).T
        inner_sum[...] = jnp.zeros_like(inner_sum)

    raw = query[...].astype(jnp.float32)
    scaled = raw * scale_cols[...]
    normed = (scaled * gain[...]).astype(jnp.bfloat16)
    keys = jnp.concatenate([key_l[...], key_c[...], key_r[...]], axis=0)
    values = jnp.concatenate([val_l[...], val_c[...], val_r[...]], axis=0)
    span = keys.shape[0] // 3
    upstream = cot[...]
    step = 128
    for start in range(0, rows, step):
        part = slice(start, start + step)
        scores = by_last(keys, normed[part]) * (FACTOR * LOG2E)
        scores = jnp.concatenate(
            [
                scores[:span] + bias[0:1, part],
                scores[span : 2 * span],
                scores[2 * span :] + bias[1:2, part],
            ],
            axis=0,
        )
        highest = jnp.max(scores, axis=0, keepdims=True)
        weights = jnp.exp2(scores - highest)
        share = 1.0 / jnp.sum(weights, axis=0, keepdims=True)
        probs_low[:, part] = (weights * share).astype(jnp.bfloat16)
        grad_probs = by_last(values, upstream[part])
        delta = jnp.sum(weights * grad_probs, axis=0, keepdims=True) * share
        grad_low[:, part] = (weights * ((grad_probs - delta) * (share * FACTOR))).astype(
            jnp.bfloat16
        )
    low = probs_low[...]
    grads = grad_low[...]
    attended[...] = plain(values.T, low).T.astype(jnp.bfloat16)
    grad = plain(keys.T, grads).T
    grad_query[...] = grad
    inner_sum[...] += raw * grad * gain[...]
    query_gain_grad[...] = jnp.sum(grad * scaled, axis=0, keepdims=True)
    grad_keys = plain(grads, normed)
    grad_values = plain(low, upstream)
    left[0] = grad_keys[:span].astype(jnp.bfloat16)
    left[1] = grad_values[:span].astype(jnp.bfloat16)
    own[0] = grad_keys[span : 2 * span]
    own[1] = grad_values[span : 2 * span]
    right[0] = grad_keys[2 * span :].astype(jnp.bfloat16)
    right[1] = grad_values[2 * span :].astype(jnp.bfloat16)
    key_gain_grad[...] = (
        jnp.sum(grad_keys * keys.astype(jnp.float32), axis=0, keepdims=True) / key_gain[...]
    )

    @pl.when(head == pl.num_programs(0) - 1)
    def _():
        inner[...] = jnp.sum(inner_sum[...].T, axis=0, keepdims=True)


def attention(bias, scale, query, cot, gain, key_gain, keys, values):
    rows, width = query.shape
    heads = width // HS
    span = keys[0].shape[0]

    def whole(shape):
        return pl.BlockSpec(shape, lambda h: (0,) * len(shape))

    def of_head(*lead):
        return pl.BlockSpec((*lead, HS), lambda h: (0,) * len(lead) + (h,))

    f32, bf16 = jnp.float32, jnp.bfloat16
    shape = jax.ShapeDtypeStruct
    return pl.pallas_call(
        attention_kernel,
        grid=(heads,),
        in_specs=[
            whole((2, rows)),
            whole((1, rows)),
            of_head(rows),
            of_head(rows),
            of_head(1),
            of_head(1),
        ]
        + [of_head(span)] * 6,
        out_specs=[
            of_head(rows),
            of_head(rows),
            whole((1, rows)),
            of_head(1),
            of_head(1),
            of_head(2, span),
            of_head(2, span),
            of_head(2, span),
        ],
        out_shape=[
            shape((rows, width), bf16),
            shape((rows, width), f32),
            shape((1, rows), f32),
            shape((1, width), f32),
            shape((1, width), f32),
            shape((2, span, width), bf16),
            shape((2, span, width), bf16),
            shape((2, span, width), f32),
        ],
        scratch_shapes=[
            pltpu.VMEM((rows, HS), f32),
            pltpu.VMEM((rows, HS), f32),
            pltpu.VMEM((3 * span, rows), bf16),
            pltpu.VMEM((3 * span, rows), bf16),
        ],
        compiler_params=pltpu.CompilerParams(vmem_limit_bytes=40 * 1024 * 1024),
        cost_estimate=pl.CostEstimate(
            flops=12 * rows * 3 * span * width, bytes_accessed=10 * rows * width, transcendentals=0
        ),
        name="attention",
    )(bias, scale, query, cot, gain, key_gain, *keys, *values)


def inverse_rms(total):
    return lax.rsqrt(total / D + EPSILON)


def shift(value, by):
    size = 1
    for axis in LINE:
        size *= lax.axis_size(axis)
    pairs = [(i, i + by) for i in range(size) if 0 <= i + by < size]
    return lax.ppermute(value, LINE, pairs)


def on_device(video_query, audio_key, audio_value, cotangent, query_gain, key_gain, time_lists):
    place = lax.axis_index(LINE)
    query_rows = video_query.astype(jnp.float32)
    key_rows = audio_key.astype(jnp.float32)
    rows = video_query.shape[0]
    value_l = shift(audio_value, 1)
    value_r = shift(audio_value, -1)
    totals = lax.psum(
        jnp.concatenate(
            [jnp.sum(query_rows * query_rows, axis=1), jnp.sum(key_rows * key_rows, axis=1)]
        ),
        "tp",
    )
    scales = inverse_rms(totals)
    query_scale = scales[:rows]
    key_scale = scales[rows:]
    key_norm = (key_rows * key_scale[:, None] * key_gain).astype(jnp.bfloat16)
    key_l = shift(key_norm, 1)
    key_r = shift(key_norm, -1)
    listed = jnp.stack(
        [jnp.any(time_lists == place - 1, axis=1), jnp.any(time_lists == place + 1, axis=1)]
    )
    bias = jnp.repeat(jnp.where(listed, 0.0, EXCLUDED).astype(jnp.float32), BLOCK, axis=1)
    (attended, grad_query, inner_query, gain_q, gain_k, to_left, to_right, own) = attention(
        bias,
        query_scale[None],
        video_query,
        cotangent,
        query_gain[None],
        key_gain[None],
        (key_l, key_norm, key_r),
        (value_l, audio_value, value_r),
    )
    from_right = shift(to_left, -1)
    from_left = shift(to_right, 1)
    gains = jnp.concatenate([gain_q, gain_k], axis=0)
    for axis in ("core", "x", "y"):
        gains = lax.psum(gains, axis)
    combined = own + from_right + from_left
    grad_key = combined[0]
    audio_value_grad = combined[1].astype(jnp.bfloat16)
    scaled_key = grad_key * key_gain
    inner = lax.psum(
        jnp.concatenate([inner_query[0], jnp.sum(key_rows * scaled_key, axis=1)]), "tp"
    )
    gains = lax.psum(gains, "far")
    shrink = scales * scales * scales * inner / D
    video_query_grad = (
        query_scale[:, None] * (grad_query * query_gain) - query_rows * shrink[:rows, None]
    ).astype(jnp.bfloat16)
    audio_key_grad = (key_scale[:, None] * scaled_key - key_rows * shrink[rows:, None]).astype(
        jnp.bfloat16
    )
    return attended, video_query_grad, audio_key_grad, audio_value_grad, gains[0], gains[1]


def solution(mesh):
    far = 4
    video, audio, tp = (mesh.shape[name] for name in ("video", "audio", "tp"))
    fine = Mesh(
        np.asarray(mesh.devices).reshape(video // far, far, audio // 2, 2, tp), (*LINE, "tp")
    )
    tokens = P(LINE, "tp")
    per_feature = P("tp")
    return jax.shard_map(
        on_device,
        mesh=fine,
        in_specs=(tokens, tokens, tokens, tokens, per_feature, per_feature, P(LINE, None)),
        out_specs=(tokens, tokens, tokens, tokens, per_feature, per_feature),
        check_vma=False,
    )
```

```python
import numpy as np
import jax
import jax.numpy as jnp
from jax import lax
from jax.experimental import pallas as pl
from jax.experimental.pallas import tpu as pltpu
from jax.sharding import Mesh, PartitionSpec as P

D = 3072
HS = 128
BLOCK = 128
FACTOR = HS ** (-0.5)
LOG2E = 1.4426950408889634
EPSILON = 1e-06
EXCLUDED = -1e30
VMEM_BYTES = 58 * 1024 * 1024
LINE = ("y", "far", "x", "core")


def by_last(left, right):
    return lax.dot_general(
        left, right, (((1,), (1,)), ((), ())), preferred_element_type=jnp.float32
    )


def plain(left, right):
    return jnp.dot(left, right, preferred_element_type=jnp.float32)


def across_rows(values):
    rows, width = values.shape
    total = values[:, :HS]
    for start in range(HS, width, HS):
        total = total + values[:, start : start + HS]
    return jnp.sum(total.T, axis=0, keepdims=True)


def as_columns(row):
    return jnp.broadcast_to(row, (HS, row.shape[1])).T


def squares_kernel(query, key, totals):
    rows = query.shape[0]
    for start in range(0, rows, BLOCK):
        part = query[start : start + BLOCK].astype(jnp.float32)
        totals[:, start : start + BLOCK] = across_rows(part * part)
    part = key[...].astype(jnp.float32)
    totals[:, rows:] = across_rows(part * part)


def squares(query, key):
    return pl.pallas_call(
        squares_kernel,
        out_shape=jax.ShapeDtypeStruct((1, query.shape[0] + key.shape[0]), jnp.float32),
        compiler_params=pltpu.CompilerParams(vmem_limit_bytes=VMEM_BYTES),
        name="squares",
    )(query, key)


def attention_kernel(
    lists, places, scale, query, cot, gain, key_gain,
    key_n, key_o, key_a, val_n, val_o, val_a,
    attended, grad_query, inner, query_gain_grad, key_gain_grad, near, across, own,
    scale_cols, inner_sum, probs_low, grad_low,
):
    head = pl.program_id(0)
    rows = query.shape[0]

    @pl.when(head == 0)
    def _():
        scale_cols[...] = as_columns(scale[...])
        inner_sum[...] = jnp.zeros_like(inner_sum)

    def closed(block, place):
        found = lists[block, 0] == place
        for entry in range(1, lists.shape[1]):
            found = jnp.logical_or(found, lists[block, entry] == place)
        return jnp.where(found, 0.0, EXCLUDED)

    raw = query[...].astype(jnp.float32)
    scaled = raw * scale_cols[...]
    normed = (scaled * gain[...]).astype(jnp.bfloat16)
    keys = jnp.concatenate([key_n[...], key_o[...], key_a[...]], axis=0)
    values = jnp.concatenate([val_n[...], val_o[...], val_a[...]], axis=0)
    span = keys.shape[0] // 3
    upstream = cot[...]
    for block in range(rows // BLOCK):
        part = slice(block * BLOCK, (block + 1) * BLOCK)
        scores = by_last(keys, normed[part]) * (FACTOR * LOG2E)
        scores = jnp.concatenate(
            [
                scores[:span] + closed(block, places[0]),
                scores[span : 2 * span],
                scores[2 * span :] + closed(block, places[1]),
            ],
            axis=0,
        )
        highest = jnp.max(scores, axis=0, keepdims=True)
        weights = jnp.exp2(scores - highest)
        share = 1.0 / jnp.sum(weights, axis=0, keepdims=True)
        probs_low[:, part] = (weights * share).astype(jnp.bfloat16)
        grad_probs = by_last(values, upstream[part])
        delta = jnp.sum(weights * grad_probs, axis=0, keepdims=True) * share
        grad_low[:, part] = (weights * ((grad_probs - delta) * (share * FACTOR))).astype(
            jnp.bfloat16
        )
    low = probs_low[...]
    grads = grad_low[...]
    attended[...] = plain(values.T, low).T.astype(jnp.bfloat16)
    grad = plain(keys.T, grads).T
    grad_query[...] = grad
    inner_sum[...] += raw * grad * gain[...]
    query_gain_grad[...] = jnp.sum(grad * scaled, axis=0, keepdims=True)
    grad_keys = plain(grads, normed)
    grad_values = plain(low, upstream)
    near[0] = grad_keys[:span].astype(jnp.bfloat16)
    near[1] = grad_values[:span].astype(jnp.bfloat16)
    own[0] = grad_keys[span : 2 * span]
    own[1] = grad_values[span : 2 * span]
    across[0] = grad_keys[2 * span :].astype(jnp.bfloat16)
    across[1] = grad_values[2 * span :].astype(jnp.bfloat16)
    key_gain_grad[...] = (
        jnp.sum(grad_keys * keys.astype(jnp.float32), axis=0, keepdims=True) / key_gain[...]
    )

    @pl.when(head == pl.num_programs(0) - 1)
    def _():
        inner[...] = across_rows(inner_sum[...])


def attention(lists, places, scale, query, cot, gain, key_gain, keys, values):
    rows, width = query.shape
    heads = width // HS
    span = keys[0].shape[0]

    def whole(shape):
        return pl.BlockSpec(shape, lambda h: (0,) * len(shape))

    def of_head(*lead):
        return pl.BlockSpec((*lead, HS), lambda h: (0,) * len(lead) + (h,))

    f32, bf16 = jnp.float32, jnp.bfloat16
    shape = jax.ShapeDtypeStruct
    scalars = pl.BlockSpec(memory_space=pltpu.SMEM)
    return pl.pallas_call(
        attention_kernel,
        grid=(heads,),
        in_specs=[scalars, scalars, whole((1, rows)), of_head(rows), of_head(rows)]
        + [of_head(1)] * 2
        + [of_head(span)] * 6,
        out_specs=[
            of_head(rows),
            of_head(rows),
            whole((1, rows)),
            of_head(1),
            of_head(1),
            of_head(2, span),
            of_head(2, span),
            of_head(2, span),
        ],
        out_shape=[
            shape((rows, width), bf16),
            shape((rows, width), f32),
            shape((1, rows), f32),
            shape((1, width), f32),
            shape((1, width), f32),
            shape((2, span, width), bf16),
            shape((2, span, width), bf16),
            shape((2, span, width), f32),
        ],
        scratch_shapes=[
            pltpu.VMEM((rows, HS), f32),
            pltpu.VMEM((rows, HS), f32),
            pltpu.VMEM((3 * span, rows), bf16),
            pltpu.VMEM((3 * span, rows), bf16),
        ],
        compiler_params=pltpu.CompilerParams(vmem_limit_bytes=VMEM_BYTES),
        cost_estimate=pl.CostEstimate(
            flops=12 * rows * 3 * span * width, bytes_accessed=10 * rows * width, transcendentals=0
        ),
        name="attention",
    )(lists, places, scale, query, cot, gain, key_gain, *keys, *values)


def combine_kernel(own, from_near, from_across, key, key_gain, grad_key, value_grad, inner):
    total = own[0] + from_near[0].astype(jnp.float32) + from_across[0].astype(jnp.float32)
    grad_key[...] = total
    value_grad[...] = (
        own[1] + from_near[1].astype(jnp.float32) + from_across[1].astype(jnp.float32)
    ).astype(jnp.bfloat16)
    inner[...] = across_rows(key[...].astype(jnp.float32) * (total * key_gain[...]))


def combine(own, from_near, from_across, key, key_gain):
    _, rows, width = own.shape
    shape = jax.ShapeDtypeStruct
    return pl.pallas_call(
        combine_kernel,
        out_shape=[
            shape((rows, width), jnp.float32),
            shape((rows, width), jnp.bfloat16),
            shape((1, rows), jnp.float32),
        ],
        compiler_params=pltpu.CompilerParams(vmem_limit_bytes=VMEM_BYTES),
        name="combine",
    )(own, from_near, from_across, key, key_gain)


def norms_backward_kernel(
    scales, inner, query, grad_query, query_gain, key, grad_key, key_gain, query_out, key_out
):
    step = pl.program_id(0)
    rows = query.shape[0]

    def one(part, raw, grad, gain):
        scale = scales[:, part]
        shrink = scale * scale * scale * inner[:, part] * (1.0 / D)
        scale, shrink = as_columns(scale), as_columns(shrink)
        pieces = []
        for start in range(0, raw.shape[1], HS):
            lanes = slice(start, start + HS)
            pieces.append(
                scale * (grad[:, lanes] * gain[:, lanes])
                - raw[:, lanes].astype(jnp.float32) * shrink
            )
        return jnp.concatenate(pieces, axis=1).astype(jnp.bfloat16)

    here = pl.ds(pl.multiple_of(step * rows, rows), rows)
    query_out[...] = one(here, query, grad_query, query_gain)

    @pl.when(step == 0)
    def _():
        first = scales.shape[1] - key.shape[0]
        key_out[...] = one(slice(first, scales.shape[1]), key, grad_key, key_gain)


def norms_backward(scales, inner, query, grad_query, query_gain, key, grad_key, key_gain):
    rows, width = query.shape

    def whole(shape):
        return pl.BlockSpec(shape, lambda i: (0,) * len(shape))

    block = pl.BlockSpec((BLOCK, width), lambda i: (i, 0))
    shape = jax.ShapeDtypeStruct
    return pl.pallas_call(
        norms_backward_kernel,
        grid=(rows // BLOCK,),
        in_specs=[
            whole(scales.shape),
            whole(inner.shape),
            block,
            block,
            whole(query_gain.shape),
            whole(key.shape),
            whole(grad_key.shape),
            whole(key_gain.shape),
        ],
        out_specs=[block, whole(key.shape)],
        out_shape=[shape(query.shape, jnp.bfloat16), shape(key.shape, jnp.bfloat16)],
        compiler_params=pltpu.CompilerParams(vmem_limit_bytes=VMEM_BYTES),
        name="norms_backward",
    )(scales, inner, query, grad_query, query_gain, key, grad_key, key_gain)


def inverse_rms(total):
    return lax.rsqrt(total / D + EPSILON)


def swap_near(value):
    return lax.ppermute(value, "core", [(0, 1), (1, 0)])


def swap_across(value):
    size = 1
    for axis in LINE:
        size *= lax.axis_size(axis)
    pairs = []
    for i in range(1, size - 1, 2):
        pairs += [(i, i + 1), (i + 1, i)]
    return lax.ppermute(value, LINE, pairs)


def on_device(video_query, audio_key, audio_value, cotangent, query_gain, key_gain, time_lists):
    place = lax.axis_index(LINE)
    core = lax.axis_index("core")
    places = jnp.stack([place + 1 - 2 * core, place - 1 + 2 * core]).astype(jnp.int32)
    rows = video_query.shape[0]
    query_gain = query_gain[None]
    key_gain = key_gain[None]
    value_n = swap_near(audio_value)
    value_a = swap_across(audio_value)
    totals = lax.psum(squares(video_query, audio_key), "tp")
    scales = inverse_rms(totals)
    key_norm = (audio_key.astype(jnp.float32) * scales[0, rows:, None] * key_gain).astype(
        jnp.bfloat16
    )
    key_norm, value_n, value_a = lax.optimization_barrier((key_norm, value_n, value_a))
    key_n = swap_near(key_norm)
    key_a = swap_across(key_norm)
    (attended, grad_query, inner_query, gain_q, gain_k, to_near, to_across, own) = attention(
        time_lists,
        places,
        scales[:, :rows],
        video_query,
        cotangent,
        query_gain,
        key_gain,
        (key_n, key_norm, key_a),
        (value_n, audio_value, value_a),
    )
    from_across = swap_across(to_across)
    from_near = swap_near(to_near)
    gains = jnp.concatenate([gain_q, gain_k], axis=0)
    for axis in ("core", "x", "y", "far"):
        gains = lax.psum(gains, axis)
    grad_key, audio_value_grad, inner_key = combine(
        own, from_near, from_across, audio_key, key_gain
    )
    inner = lax.psum(jnp.concatenate([inner_query, inner_key], axis=1), "tp")
    video_query_grad, audio_key_grad = norms_backward(
        scales, inner, video_query, grad_query, query_gain, audio_key, grad_key, key_gain
    )
    return attended, video_query_grad, audio_key_grad, audio_value_grad, gains[0], gains[1]


def solution(mesh):
    far = 4
    video, audio, tp = (mesh.shape[name] for name in ("video", "audio", "tp"))
    fine = Mesh(
        np.asarray(mesh.devices).reshape(video // far, far, audio // 2, 2, tp), (*LINE, "tp")
    )
    tokens = P(LINE, "tp")
    per_feature = P("tp")
    return jax.shard_map(
        on_device,
        mesh=fine,
        in_specs=(tokens, tokens, tokens, tokens, per_feature, per_feature, P(LINE, None)),
        out_specs=(tokens, tokens, tokens, tokens, per_feature, per_feature),
        check_vma=False,
    )
```

```python
import numpy as np
import jax
import jax.numpy as jnp
from jax import lax
from jax.experimental import pallas as pl
from jax.experimental.pallas import tpu as pltpu
from jax.sharding import Mesh, PartitionSpec as P

D = 3072
HS = 128
BLOCK = 128
FACTOR = HS ** (-0.5)
LOG2E = 1.4426950408889634
EPSILON = 1e-06
EXCLUDED = -1e30
VMEM_BYTES = 58 * 1024 * 1024
LINE = ("y", "far", "x", "core")


def by_last(left, right):
    return lax.dot_general(
        left, right, (((1,), (1,)), ((), ())), preferred_element_type=jnp.float32
    )


def plain(left, right):
    return jnp.dot(left, right, preferred_element_type=jnp.float32)


def across_rows(values):
    rows, width = values.shape
    total = values[:, :HS]
    for start in range(HS, width, HS):
        total = total + values[:, start : start + HS]
    return jnp.sum(total.T, axis=0, keepdims=True)


def as_columns(row):
    return jnp.broadcast_to(row, (HS, row.shape[1])).T


def inverse_rms(total):
    return lax.rsqrt(total * (1.0 / D) + EPSILON)


def squares_kernel(query, key, totals):
    rows = query.shape[0]
    for start in range(0, rows, BLOCK):
        part = query[start : start + BLOCK].astype(jnp.float32)
        totals[:, start : start + BLOCK] = across_rows(part * part)
    part = key[...].astype(jnp.float32)
    totals[:, rows:] = across_rows(part * part)


def squares(query, key):
    return pl.pallas_call(
        squares_kernel,
        out_shape=jax.ShapeDtypeStruct((1, query.shape[0] + key.shape[0]), jnp.float32),
        compiler_params=pltpu.CompilerParams(vmem_limit_bytes=VMEM_BYTES),
        name="squares",
    )(query, key)


def attention_kernel(
    lists, places, totals, totals_n, totals_a, query, cot, gain, key_gain, own_key, own_value,
    halo_n, halo_a,
    attended, grad_query, inner, gains, near, across, own,
    scale_cols, key_cols, inner_sum, probs_low, grad_low,
):
    head = pl.program_id(0)
    rows = query.shape[0]
    span = own_key.shape[0]

    @pl.when(head == 0)
    def _():
        scale_cols[...] = as_columns(inverse_rms(totals[:, :rows]))
        for index, source in enumerate((totals_n, totals, totals_a)):
            key_cols[index * span : (index + 1) * span] = as_columns(
                inverse_rms(source[:, rows:])
            )
        inner_sum[...] = jnp.zeros_like(inner_sum)

    def closed(block, place):
        found = lists[block, 0] == place
        for entry in range(1, lists.shape[1]):
            found = jnp.logical_or(found, lists[block, entry] == place)
        return jnp.where(found, 0.0, EXCLUDED)

    raw = query[...].astype(jnp.float32)
    scaled = raw * scale_cols[...]
    normed = (scaled * gain[...]).astype(jnp.bfloat16)
    key_raw = jnp.concatenate([halo_n[0], own_key[...], halo_a[0]], axis=0)
    values = jnp.concatenate([halo_n[1], own_value[...], halo_a[1]], axis=0)
    key_scaled = key_raw.astype(jnp.float32) * key_cols[...]
    keys = (key_scaled * key_gain[...]).astype(jnp.bfloat16)
    upstream = cot[...]
    for block in range(rows // BLOCK):
        part = slice(block * BLOCK, (block + 1) * BLOCK)
        scores = by_last(keys, normed[part]) * (FACTOR * LOG2E)
        scores = jnp.concatenate(
            [
                scores[:span] + closed(block, places[0]),
                scores[span : 2 * span],
                scores[2 * span :] + closed(block, places[1]),
            ],
            axis=0,
        )
        highest = jnp.max(scores, axis=0, keepdims=True)
        weights = jnp.exp2(scores - highest)
        share = 1.0 / jnp.sum(weights, axis=0, keepdims=True)
        probs_low[:, part] = (weights * share).astype(jnp.bfloat16)
        grad_probs = by_last(values, upstream[part])
        delta = jnp.sum(weights * grad_probs, axis=0, keepdims=True) * share
        grad_low[:, part] = (weights * ((grad_probs - delta) * (share * FACTOR))).astype(
            jnp.bfloat16
        )
    low = probs_low[...]
    grads = grad_low[...]
    attended[...] = plain(values.T, low).T.astype(jnp.bfloat16)
    grad = plain(keys.T, grads).T
    grad_query[...] = grad
    inner_sum[...] += raw * grad * gain[...]
    grad_keys = plain(grads, normed)
    grad_values = plain(low, upstream)
    gains[0:1] = jnp.sum(grad * scaled, axis=0, keepdims=True)
    gains[1:2] = jnp.sum(grad_keys * key_scaled, axis=0, keepdims=True)
    near[0] = grad_keys[:span].astype(jnp.bfloat16)
    near[1] = grad_values[:span].astype(jnp.bfloat16)
    own[0] = grad_keys[span : 2 * span]
    own[1] = grad_values[span : 2 * span]
    across[0] = grad_keys[2 * span :].astype(jnp.bfloat16)
    across[1] = grad_values[2 * span :].astype(jnp.bfloat16)

    @pl.when(head == pl.num_programs(0) - 1)
    def _():
        inner[...] = across_rows(inner_sum[...])


def attention(
    lists, places, totals, totals_n, totals_a, query, cot, gain, key_gain, key, value, halo_n, halo_a
):
    rows, width = query.shape
    heads = width // HS
    span = key.shape[0]

    def whole(shape):
        return pl.BlockSpec(shape, lambda h: (0,) * len(shape))

    def of_head(*lead):
        return pl.BlockSpec((*lead, HS), lambda h: (0,) * len(lead) + (h,))

    f32, bf16 = jnp.float32, jnp.bfloat16
    shape = jax.ShapeDtypeStruct
    scalars = pl.BlockSpec(memory_space=pltpu.SMEM)
    return pl.pallas_call(
        attention_kernel,
        grid=(heads,),
        in_specs=[scalars] * 2
        + [whole(totals.shape)] * 3
        + [of_head(rows)] * 2
        + [of_head(1)] * 2
        + [of_head(span)] * 2
        + [of_head(2, span)] * 2,
        out_specs=[
            of_head(rows),
            of_head(rows),
            whole((1, rows)),
            of_head(2),
            of_head(2, span),
            of_head(2, span),
            of_head(2, span),
        ],
        out_shape=[
            shape((rows, width), bf16),
            shape((rows, width), f32),
            shape((1, rows), f32),
            shape((2, width), f32),
            shape((2, span, width), bf16),
            shape((2, span, width), bf16),
            shape((2, span, width), f32),
        ],
        scratch_shapes=[
            pltpu.VMEM((rows, HS), f32),
            pltpu.VMEM((3 * span, HS), f32),
            pltpu.VMEM((rows, HS), f32),
            pltpu.VMEM((3 * span, rows), bf16),
            pltpu.VMEM((3 * span, rows), bf16),
        ],
        compiler_params=pltpu.CompilerParams(vmem_limit_bytes=VMEM_BYTES),
        cost_estimate=pl.CostEstimate(
            flops=12 * rows * 3 * span * width, bytes_accessed=10 * rows * width, transcendentals=0
        ),
        name="attention",
    )(lists, places, totals, totals_n, totals_a, query, cot, gain, key_gain, key, value, halo_n, halo_a)


def combine_kernel(
    own, from_near, from_across, key, key_gain, inner_query, grad_key, value_grad, inner
):
    total = own[0] + from_near[0].astype(jnp.float32) + from_across[0].astype(jnp.float32)
    grad_key[...] = total
    value_grad[...] = (
        own[1] + from_near[1].astype(jnp.float32) + from_across[1].astype(jnp.float32)
    ).astype(jnp.bfloat16)
    rows = inner_query.shape[1]
    inner[:, :rows] = inner_query[...]
    inner[:, rows:] = across_rows(key[...].astype(jnp.float32) * (total * key_gain[...]))


def combine(own, from_near, from_across, key, key_gain, inner_query):
    _, rows, width = own.shape
    shape = jax.ShapeDtypeStruct
    return pl.pallas_call(
        combine_kernel,
        out_shape=[
            shape((rows, width), jnp.float32),
            shape((rows, width), jnp.bfloat16),
            shape((1, inner_query.shape[1] + rows), jnp.float32),
        ],
        compiler_params=pltpu.CompilerParams(vmem_limit_bytes=VMEM_BYTES),
        name="combine",
    )(own, from_near, from_across, key, key_gain, inner_query)


def norms_backward_kernel(
    totals, inner_parts, gains, query, grad_query, query_gain, key, grad_key, key_gain,
    query_out, key_out, query_gain_grad, key_gain_grad,
):
    rows = query.shape[0]
    inner = inner_parts[0]
    for index in range(1, len(inner_parts)):
        inner = inner + inner_parts[index]
    scale = inverse_rms(totals[...])
    shrink = scale * scale * scale * inner * (1.0 / D)

    def one(start, out, raw, grad, gain):
        here = slice(start, start + BLOCK)
        wide, less = as_columns(scale[:, here]), as_columns(shrink[:, here])
        first = start % rows
        there = slice(first, first + BLOCK)
        for lane in range(0, raw.shape[1], HS):
            lanes = slice(lane, lane + HS)
            out[there, lanes] = (
                wide * (grad[there, lanes] * gain[:, lanes])
                - raw[there, lanes].astype(jnp.float32) * less
            ).astype(jnp.bfloat16)

    for start in range(0, rows, BLOCK):
        one(start, query_out, query, grad_query, query_gain)
    one(rows, key_out, key, grad_key, key_gain)
    query_gain_grad[...] = gains[0:1]
    key_gain_grad[...] = gains[1:2]


def norms_backward(totals, inner_parts, gains, *rest):
    query, key = rest[0], rest[3]
    count = len(inner_parts)

    def kernel(totals, *refs):
        parts = [ref[...] for ref in refs[:count]]
        norms_backward_kernel(totals, parts, *refs[count:])

    shape = jax.ShapeDtypeStruct
    width = query.shape[1]
    return pl.pallas_call(
        kernel,
        out_shape=[
            shape(query.shape, jnp.bfloat16),
            shape(key.shape, jnp.bfloat16),
            shape((1, width), jnp.float32),
            shape((1, width), jnp.float32),
        ],
        compiler_params=pltpu.CompilerParams(vmem_limit_bytes=VMEM_BYTES),
        name="norms_backward",
    )(totals, *inner_parts, gains, *rest)


def swap_near(value):
    return lax.ppermute(value, "core", [(0, 1), (1, 0)])


def swap_across(value):
    size = 1
    for axis in LINE:
        size *= lax.axis_size(axis)
    pairs = []
    for i in range(1, size - 1, 2):
        pairs += [(i, i + 1), (i + 1, i)]
    return lax.ppermute(value, LINE, pairs)


def on_device(video_query, audio_key, audio_value, cotangent, query_gain, key_gain, time_lists):
    place = lax.axis_index(LINE)
    core = lax.axis_index("core")
    places = jnp.stack([place + 1 - 2 * core, place - 1 + 2 * core]).astype(jnp.int32)
    query_gain = query_gain[None]
    key_gain = key_gain[None]
    held = jnp.stack([audio_key, audio_value])
    halo_a = swap_across(held)
    halo_n = swap_near(held)
    totals = lax.psum(squares(video_query, audio_key), "tp")
    totals_a = swap_across(totals)
    totals_n = swap_near(totals)
    (attended, grad_query, inner_query, gains, to_near, to_across, own) = attention(
        time_lists,
        places,
        totals,
        totals_n,
        totals_a,
        video_query,
        cotangent,
        query_gain,
        key_gain,
        audio_key,
        audio_value,
        halo_n,
        halo_a,
    )
    from_across = swap_across(to_across)
    from_near = swap_near(to_near)
    for axis in ("core", "x", "y"):
        gains = lax.psum(gains, axis)
    grad_key, audio_value_grad, inner = combine(
        own, from_near, from_across, audio_key, key_gain, inner_query
    )
    inner, gains = lax.optimization_barrier((inner, gains))
    size = lax.axis_size("tp")
    inner_parts = [inner] + [
        lax.ppermute(inner, "tp", [(i, (i + by) % size) for i in range(size)])
        for by in range(1, size)
    ]
    gains = lax.psum(gains, "far")
    video_query_grad, audio_key_grad, query_gain_grad, key_gain_grad = norms_backward(
        totals,
        inner_parts,
        gains,
        video_query,
        grad_query,
        query_gain,
        audio_key,
        grad_key,
        key_gain,
    )
    return (
        attended,
        video_query_grad,
        audio_key_grad,
        audio_value_grad,
        query_gain_grad[0],
        key_gain_grad[0],
    )


def solution(mesh):
    far = 4
    video, audio, tp = (mesh.shape[name] for name in ("video", "audio", "tp"))
    fine = Mesh(
        np.asarray(mesh.devices).reshape(video // far, far, audio // 2, 2, tp), (*LINE, "tp")
    )
    tokens = P(LINE, "tp")
    per_feature = P("tp")
    return jax.shard_map(
        on_device,
        mesh=fine,
        in_specs=(tokens, tokens, tokens, tokens, per_feature, per_feature, P(LINE, None)),
        out_specs=(tokens, tokens, tokens, tokens, per_feature, per_feature),
        check_vma=False,
    )
```

```python
import numpy as np
import jax
import jax.numpy as jnp
from jax import lax
from jax.experimental import pallas as pl
from jax.experimental.pallas import tpu as pltpu
from jax.sharding import Mesh, PartitionSpec as P

D = 3072
HS = 128
BLOCK = 128
FACTOR = HS ** (-0.5)
LOG2E = 1.4426950408889634
EPSILON = 1e-06
EXCLUDED = -1e30
VMEM_BYTES = 24 * 1024 * 1024
LINE = ("y", "far", "x", "core")


def by_last(left, right):
    return lax.dot_general(
        left, right, (((1,), (1,)), ((), ())), preferred_element_type=jnp.float32
    )


def plain(left, right):
    return jnp.dot(left, right, preferred_element_type=jnp.float32)


def across_rows(values):
    rows, width = values.shape
    total = values[:, :HS]
    for start in range(HS, width, HS):
        total = total + values[:, start : start + HS]
    return jnp.sum(total.T, axis=0, keepdims=True)


def as_columns(row):
    return jnp.broadcast_to(row, (HS, row.shape[1])).T


def inverse_rms(total):
    return lax.rsqrt(total * (1.0 / D) + EPSILON)


def squares_kernel(query, key, totals):
    rows = query.shape[0]
    for start in range(0, rows, BLOCK):
        part = query[start : start + BLOCK].astype(jnp.float32)
        totals[:, start : start + BLOCK] = across_rows(part * part)
    part = key[...].astype(jnp.float32)
    totals[:, rows:] = across_rows(part * part)


def squares(query, key):
    return pl.pallas_call(
        squares_kernel,
        out_shape=jax.ShapeDtypeStruct((1, query.shape[0] + key.shape[0]), jnp.float32),
        compiler_params=pltpu.CompilerParams(vmem_limit_bytes=VMEM_BYTES),
        name="squares",
    )(query, key)


def attention_kernel(
    lists, places, totals, totals_n, totals_a, query, cot, gain, key_gain, own_key, own_value,
    halo_n, halo_a,
    attended, grad_query, inner, gains, near, across, own,
    scale_cols, key_cols, inner_sum, probs_low, grad_low,
):
    head = pl.program_id(0)
    rows = query.shape[0]
    span = own_key.shape[0]

    @pl.when(head == 0)
    def _():
        scale_cols[...] = as_columns(inverse_rms(totals[:, :rows]))
        for index, source in enumerate((totals_n, totals, totals_a)):
            key_cols[index * span : (index + 1) * span] = as_columns(
                inverse_rms(source[:, rows:])
            )
        inner_sum[...] = jnp.zeros_like(inner_sum)

    def closed(block, place):
        found = lists[block, 0] == place
        for entry in range(1, lists.shape[1]):
            found = jnp.logical_or(found, lists[block, entry] == place)
        return jnp.where(found, 0.0, EXCLUDED)

    def soften(lanes, slot, keys, values, normed, upstream, blocks):
        part = slice(blocks[0] * BLOCK, (blocks[-1] + 1) * BLOCK)
        scores = by_last(keys, normed[part])
        scores = jnp.concatenate(
            [scores[:span] + shut(blocks, 0), scores[span : 2 * span], scores[2 * span :] + shut(blocks, 1)],
            axis=0,
        )
        highest = jnp.max(scores, axis=0, keepdims=True)
        weights = jnp.exp2((scores - highest) * (FACTOR * LOG2E))
        share = 1.0 / jnp.sum(weights, axis=0, keepdims=True)
        probs_low[slot, :, part] = (weights * share).astype(jnp.bfloat16)
        grad_probs = by_last(values, upstream[part])
        delta = jnp.sum(weights * grad_probs, axis=0, keepdims=True) * share
        grad_low[slot, :, part] = (weights * ((grad_probs - delta) * (share * FACTOR))).astype(
            jnp.bfloat16
        )

    def shut(blocks, side):
        if len(blocks) == 1:
            return closed(blocks[0], places[side])
        return jnp.concatenate([jnp.full((1, BLOCK), closed(b, places[side])) for b in blocks], axis=1)

    def prepare(slot):
        lanes = slice(slot * HS, (slot + 1) * HS)
        raw = query[:, lanes].astype(jnp.float32)
        scaled = raw * scale_cols[...]
        normed = (scaled * gain[:, lanes]).astype(jnp.bfloat16)
        key_raw = jnp.concatenate([halo_n[0, :, lanes], own_key[:, lanes], halo_a[0, :, lanes]], axis=0)
        values = jnp.concatenate([halo_n[1, :, lanes], own_value[:, lanes], halo_a[1, :, lanes]], axis=0)
        key_scaled = key_raw.astype(jnp.float32) * key_cols[...]
        keys = (key_scaled * key_gain[:, lanes]).astype(jnp.bfloat16)
        return lanes, raw, scaled, normed, values, key_scaled, keys, cot[:, lanes]

    def finish(slot, lanes, raw, scaled, normed, values, key_scaled, keys, upstream):
        low = probs_low[slot]
        grads = grad_low[slot]
        attended[:, lanes] = plain(values.T, low).T.astype(jnp.bfloat16)
        grad = plain(keys.T, grads).T
        grad_query[:, lanes] = grad
        inner_sum[...] += raw * grad * gain[:, lanes]
        grad_keys = plain(grads, normed)
        grad_values = plain(low, upstream)
        gains[0:1, lanes] = jnp.sum(grad * scaled, axis=0, keepdims=True)
        gains[1:2, lanes] = jnp.sum(grad_keys * key_scaled, axis=0, keepdims=True)
        near[0, :, lanes] = grad_keys[:span].astype(jnp.bfloat16)
        near[1, :, lanes] = grad_values[:span].astype(jnp.bfloat16)
        own[0, :, lanes] = grad_keys[span : 2 * span]
        own[1, :, lanes] = grad_values[span : 2 * span]
        across[0, :, lanes] = grad_keys[2 * span :].astype(jnp.bfloat16)
        across[1, :, lanes] = grad_values[2 * span :].astype(jnp.bfloat16)

    total = rows // BLOCK
    groups = [list(range(i, min(i + 2, total))) for i in range(0, total, 2)]
    held = [prepare(slot) for slot in range(2)]
    for slot in range(2):
        lanes, raw, scaled, normed, values, key_scaled, keys, upstream = held[slot]
        for blocks in groups:
            soften(lanes, slot, keys, values, normed, upstream, blocks)
        if slot and 1 == 1:
            finish(slot - 1, *held[slot - 1])
        if 1 == 0:
            finish(slot, *held[slot])
    if 1 == 1:
        finish(2 - 1, *held[-1])

    @pl.when(head == pl.num_programs(0) - 1)
    def _():
        inner[...] = across_rows(inner_sum[...])


def attention(
    lists, places, totals, totals_n, totals_a, query, cot, gain, key_gain, key, value, halo_n, halo_a
):
    rows, width = query.shape
    heads = width // (2 * HS)
    span = key.shape[0]

    def whole(shape):
        return pl.BlockSpec(shape, lambda h: (0,) * len(shape))

    def of_head(*lead):
        return pl.BlockSpec((*lead, 2 * HS), lambda h: (0,) * len(lead) + (h,))

    f32, bf16 = jnp.float32, jnp.bfloat16
    shape = jax.ShapeDtypeStruct
    scalars = pl.BlockSpec(memory_space=pltpu.SMEM)
    return pl.pallas_call(
        attention_kernel,
        grid=(heads,),
        in_specs=[scalars] * 2
        + [whole(totals.shape)] * 3
        + [of_head(rows)] * 2
        + [of_head(1)] * 2
        + [of_head(span)] * 2
        + [of_head(2, span)] * 2,
        out_specs=[
            of_head(rows),
            of_head(rows),
            whole((1, rows)),
            of_head(2),
            of_head(2, span),
            of_head(2, span),
            of_head(2, span),
        ],
        out_shape=[
            shape((rows, width), bf16),
            shape((rows, width), f32),
            shape((1, rows), f32),
            shape((2, width), f32),
            shape((2, span, width), bf16),
            shape((2, span, width), bf16),
            shape((2, span, width), f32),
        ],
        scratch_shapes=[
            pltpu.VMEM((rows, HS), f32),
            pltpu.VMEM((3 * span, HS), f32),
            pltpu.VMEM((rows, HS), f32),
            pltpu.VMEM((2, 3 * span, rows), bf16),
            pltpu.VMEM((2, 3 * span, rows), bf16),
        ],
        compiler_params=pltpu.CompilerParams(vmem_limit_bytes=VMEM_BYTES),
        cost_estimate=pl.CostEstimate(
            flops=12 * rows * 3 * span * width, bytes_accessed=10 * rows * width, transcendentals=0
        ),
        name="attention",
    )(lists, places, totals, totals_n, totals_a, query, cot, gain, key_gain, key, value, halo_n, halo_a)


def combine_kernel(
    own, from_near, from_across, key, key_gain, inner_query, grad_key, value_grad, inner
):
    total = own[0] + from_near[0].astype(jnp.float32) + from_across[0].astype(jnp.float32)
    grad_key[...] = total
    value_grad[...] = (
        own[1] + from_near[1].astype(jnp.float32) + from_across[1].astype(jnp.float32)
    ).astype(jnp.bfloat16)
    rows = inner_query.shape[1]
    inner[:, :rows] = inner_query[...]
    inner[:, rows:] = across_rows(key[...].astype(jnp.float32) * (total * key_gain[...]))


def combine(own, from_near, from_across, key, key_gain, inner_query):
    _, rows, width = own.shape
    shape = jax.ShapeDtypeStruct
    return pl.pallas_call(
        combine_kernel,
        out_shape=[
            shape((rows, width), jnp.float32),
            shape((rows, width), jnp.bfloat16),
            shape((1, inner_query.shape[1] + rows), jnp.float32),
        ],
        compiler_params=pltpu.CompilerParams(vmem_limit_bytes=VMEM_BYTES),
        name="combine",
    )(own, from_near, from_across, key, key_gain, inner_query)


def norms_backward_kernel(
    totals, inner_parts, gains, query, grad_query, query_gain, key, grad_key, key_gain,
    query_out, key_out, query_gain_grad, key_gain_grad,
):
    rows = query.shape[0]
    inner = inner_parts[0]
    for index in range(1, len(inner_parts)):
        inner = inner + inner_parts[index]
    scale = inverse_rms(totals[...])
    shrink = scale * scale * scale * inner * (1.0 / D)

    def one(start, out, raw, grad, gain):
        here = slice(start, start + BLOCK)
        wide, less = as_columns(scale[:, here]), as_columns(shrink[:, here])
        first = start % rows
        there = slice(first, first + BLOCK)
        for lane in range(0, raw.shape[1], HS):
            lanes = slice(lane, lane + HS)
            out[there, lanes] = (
                wide * (grad[there, lanes] * gain[:, lanes])
                - raw[there, lanes].astype(jnp.float32) * less
            ).astype(jnp.bfloat16)

    for start in range(0, rows, BLOCK):
        one(start, query_out, query, grad_query, query_gain)
    one(rows, key_out, key, grad_key, key_gain)
    query_gain_grad[...] = gains[0]
    key_gain_grad[...] = gains[1]


def norms_backward(totals, inner_parts, gains, *rest):
    query, key = rest[0], rest[3]
    count = len(inner_parts)

    def kernel(totals, *refs):
        parts = [ref[...] for ref in refs[:count]]
        norms_backward_kernel(totals, parts, *refs[count:])

    shape = jax.ShapeDtypeStruct
    width = query.shape[1]
    return pl.pallas_call(
        kernel,
        out_shape=[
            shape(query.shape, jnp.bfloat16),
            shape(key.shape, jnp.bfloat16),
            shape((width,), jnp.float32),
            shape((width,), jnp.float32),
        ],
        compiler_params=pltpu.CompilerParams(vmem_limit_bytes=VMEM_BYTES),
        name="norms_backward",
    )(totals, *inner_parts, gains, *rest)


def swap_near(value):
    return lax.ppermute(value, "core", [(0, 1), (1, 0)])


def swap_across(value):
    size = 1
    for axis in LINE:
        size *= lax.axis_size(axis)
    pairs = []
    for i in range(1, size - 1, 2):
        pairs += [(i, i + 1), (i + 1, i)]
    return lax.ppermute(value, LINE, pairs)


def on_device(video_query, audio_key, audio_value, cotangent, query_gain, key_gain, time_lists):
    place = lax.axis_index(LINE)
    core = lax.axis_index("core")
    places = jnp.stack([place + 1 - 2 * core, place - 1 + 2 * core]).astype(jnp.int32)
    query_gain = query_gain[None]
    key_gain = key_gain[None]
    own_parts = squares(video_query, audio_key)
    parts_a = swap_across(own_parts)
    parts_n = swap_near(own_parts)
    held = jnp.stack([audio_key, audio_value])
    held, parts_a, parts_n = lax.optimization_barrier((held, parts_a, parts_n))
    halo_a = swap_across(held)
    halo_n = swap_near(held)
    totals, totals_n, totals_a = lax.psum((own_parts, parts_n, parts_a), "tp")
    (attended, grad_query, inner_query, gains, to_near, to_across, own) = attention(
        time_lists,
        places,
        totals,
        totals_n,
        totals_a,
        video_query,
        cotangent,
        query_gain,
        key_gain,
        audio_key,
        audio_value,
        halo_n,
        halo_a,
    )
    from_across = swap_across(to_across)
    from_near = swap_near(to_near)
    for axis in ("core", "x", "y"):
        gains = lax.psum(gains, axis)
    grad_key, audio_value_grad, inner = combine(
        own, from_near, from_across, audio_key, key_gain, inner_query
    )
    inner, gains = lax.optimization_barrier((inner, gains))
    size = lax.axis_size("tp")
    inner_parts = [inner] + [
        lax.ppermute(inner, "tp", [(i, (i + by) % size) for i in range(size)])
        for by in range(1, size)
    ]
    gains = lax.psum(gains, "far")
    video_query_grad, audio_key_grad, query_gain_grad, key_gain_grad = norms_backward(
        totals,
        inner_parts,
        gains,
        video_query,
        grad_query,
        query_gain,
        audio_key,
        grad_key,
        key_gain,
    )
    return (
        attended,
        video_query_grad,
        audio_key_grad,
        audio_value_grad,
        query_gain_grad,
        key_gain_grad,
    )


def solution(mesh):
    far = 4
    video, audio, tp = (mesh.shape[name] for name in ("video", "audio", "tp"))
    fine = Mesh(
        np.asarray(mesh.devices).reshape(video // far, far, audio // 2, 2, tp), (*LINE, "tp")
    )
    tokens = P(LINE, "tp")
    per_feature = P("tp")
    return jax.shard_map(
        on_device,
        mesh=fine,
        in_specs=(tokens, tokens, tokens, tokens, per_feature, per_feature, P(LINE, None)),
        out_specs=(tokens, tokens, tokens, tokens, per_feature, per_feature),
        check_vma=False,
    )
```

```python
import numpy as np
import jax
import jax.numpy as jnp
from jax import lax
from jax.experimental import pallas as pl
from jax.experimental.pallas import tpu as pltpu
from jax.sharding import Mesh, PartitionSpec as P

D = 3072
HS = 128
BLOCK = 128
FACTOR = HS ** (-0.5)
LOG2E = 1.4426950408889634
EPSILON = 1e-06
EXCLUDED = -1e30
VMEM_BYTES = 24 * 1024 * 1024
LINE = ("y", "far", "x", "core")


def by_last(left, right):
    return lax.dot_general(
        left, right, (((1,), (1,)), ((), ())), preferred_element_type=jnp.float32
    )


def plain(left, right):
    return jnp.dot(left, right, preferred_element_type=jnp.float32)


def across_rows(values):
    rows, width = values.shape
    total = values[:, :HS]
    for start in range(HS, width, HS):
        total = total + values[:, start : start + HS]
    return jnp.sum(total.T, axis=0, keepdims=True)


def as_columns(row):
    return jnp.broadcast_to(row, (HS, row.shape[1])).T


def inverse_rms(total):
    return lax.rsqrt(total * (1.0 / D) + EPSILON)


def squares_kernel(query, key, totals):
    rows = query.shape[0]
    for start in range(0, rows, BLOCK):
        part = query[start : start + BLOCK].astype(jnp.float32)
        totals[:, start : start + BLOCK] = across_rows(part * part)
    part = key[...].astype(jnp.float32)
    totals[:, rows:] = across_rows(part * part)


def squares(query, key):
    return pl.pallas_call(
        squares_kernel,
        out_shape=jax.ShapeDtypeStruct((1, query.shape[0] + key.shape[0]), jnp.float32),
        compiler_params=pltpu.CompilerParams(vmem_limit_bytes=VMEM_BYTES),
        name="squares",
    )(query, key)


def norm_keys_kernel(totals, key, value, gain, held):
    first = totals.shape[1] - key.shape[0]
    scale = as_columns(inverse_rms(totals[:, first:]))
    for start in range(0, key.shape[1], HS):
        lanes = slice(start, start + HS)
        held[0, :, lanes] = (key[:, lanes].astype(jnp.float32) * scale * gain[:, lanes]).astype(
            jnp.bfloat16
        )
    held[1] = value[...]


def norm_keys(totals, key, value, gain):
    return pl.pallas_call(
        norm_keys_kernel,
        out_shape=jax.ShapeDtypeStruct((2, *key.shape), jnp.bfloat16),
        compiler_params=pltpu.CompilerParams(vmem_limit_bytes=VMEM_BYTES),
        name="norm_keys",
    )(totals, key, value, gain)


def attention_kernel(
    lists, places, totals, query, cot, gain, key_gain, held, halo_n, halo_a,
    attended, grad_query, inner, gains, near, across, own,
    scale_cols, inner_sum, probs_low, grad_low,
):
    head = pl.program_id(0)
    rows = query.shape[0]
    span = held.shape[1]

    @pl.when(head == 0)
    def _():
        scale_cols[...] = as_columns(inverse_rms(totals[:, :rows]))
        inner_sum[...] = jnp.zeros_like(inner_sum)

    def closed(block, place):
        found = lists[block, 0] == place
        for entry in range(1, lists.shape[1]):
            found = jnp.logical_or(found, lists[block, entry] == place)
        return jnp.where(found, 0.0, EXCLUDED)

    def soften(lanes, slot, keys, values, normed, upstream, blocks):
        part = slice(blocks[0] * BLOCK, (blocks[-1] + 1) * BLOCK)
        scores = by_last(keys, normed[part])
        scores = jnp.concatenate(
            [scores[:span] + shut(blocks, 0), scores[span : 2 * span], scores[2 * span :] + shut(blocks, 1)],
            axis=0,
        )
        highest = jnp.max(scores, axis=0, keepdims=True)
        weights = jnp.exp2((scores - highest) * (FACTOR * LOG2E))
        share = 1.0 / jnp.sum(weights, axis=0, keepdims=True)
        probs_low[slot, :, part] = (weights * share).astype(jnp.bfloat16)
        grad_probs = by_last(values, upstream[part])
        delta = jnp.sum(weights * grad_probs, axis=0, keepdims=True) * share
        grad_low[slot, :, part] = (weights * ((grad_probs - delta) * (share * FACTOR))).astype(
            jnp.bfloat16
        )

    def shut(blocks, side):
        if len(blocks) == 1:
            return closed(blocks[0], places[side])
        return jnp.concatenate([jnp.full((1, BLOCK), closed(b, places[side])) for b in blocks], axis=1)

    def prepare(slot):
        lanes = slice(slot * HS, (slot + 1) * HS)
        raw = query[:, lanes].astype(jnp.float32)
        scaled = raw * scale_cols[...]
        normed = (scaled * gain[:, lanes]).astype(jnp.bfloat16)
        keys = jnp.concatenate([halo_n[0, :, lanes], held[0, :, lanes], halo_a[0, :, lanes]], axis=0)
        values = jnp.concatenate([halo_n[1, :, lanes], held[1, :, lanes], halo_a[1, :, lanes]], axis=0)
        return lanes, raw, scaled, normed, values, keys, cot[:, lanes]

    def finish(slot, lanes, raw, scaled, normed, values, keys, upstream):
        low = probs_low[slot]
        grads = grad_low[slot]
        attended[:, lanes] = plain(values.T, low).T.astype(jnp.bfloat16)
        grad = plain(keys.T, grads).T
        grad_query[:, lanes] = grad
        inner_sum[...] += raw * grad * gain[:, lanes]
        grad_keys = plain(grads, normed)
        grad_values = plain(low, upstream)
        gains[0:1, lanes] = jnp.sum(grad * scaled, axis=0, keepdims=True)
        gains[1:2, lanes] = (
            jnp.sum(grad_keys * keys.astype(jnp.float32), axis=0, keepdims=True)
            / key_gain[:, lanes]
        )
        near[0, :, lanes] = grad_keys[:span].astype(jnp.bfloat16)
        near[1, :, lanes] = grad_values[:span].astype(jnp.bfloat16)
        own[0, :, lanes] = grad_keys[span : 2 * span]
        own[1, :, lanes] = grad_values[span : 2 * span]
        across[0, :, lanes] = grad_keys[2 * span :].astype(jnp.bfloat16)
        across[1, :, lanes] = grad_values[2 * span :].astype(jnp.bfloat16)

    total = rows // BLOCK
    groups = [list(range(i, min(i + 2, total))) for i in range(0, total, 2)]
    ready = [prepare(slot) for slot in range(2)]
    for slot in range(2):
        lanes, raw, scaled, normed, values, keys, upstream = ready[slot]
        for blocks in groups:
            soften(lanes, slot, keys, values, normed, upstream, blocks)
        if slot and 1 == 1:
            finish(slot - 1, *ready[slot - 1])
        if 1 == 0:
            finish(slot, *ready[slot])
    if 1 == 1:
        finish(2 - 1, *ready[-1])

    @pl.when(head == pl.num_programs(0) - 1)
    def _():
        inner[...] = across_rows(inner_sum[...])


def attention(lists, places, totals, query, cot, gain, key_gain, held, halo_n, halo_a):
    rows, width = query.shape
    heads = width // (2 * HS)
    span = held.shape[1]

    def whole(shape):
        return pl.BlockSpec(shape, lambda h: (0,) * len(shape))

    def of_head(*lead):
        return pl.BlockSpec((*lead, 2 * HS), lambda h: (0,) * len(lead) + (h,))

    f32, bf16 = jnp.float32, jnp.bfloat16
    shape = jax.ShapeDtypeStruct
    scalars = pl.BlockSpec(memory_space=pltpu.SMEM)
    return pl.pallas_call(
        attention_kernel,
        grid=(heads,),
        in_specs=[scalars] * 2
        + [whole(totals.shape)]
        + [of_head(rows)] * 2
        + [of_head(1)] * 2
        + [of_head(2, span)] * 3,
        out_specs=[
            of_head(rows),
            of_head(rows),
            whole((1, rows)),
            of_head(2),
            of_head(2, span),
            of_head(2, span),
            of_head(2, span),
        ],
        out_shape=[
            shape((rows, width), bf16),
            shape((rows, width), f32),
            shape((1, rows), f32),
            shape((2, width), f32),
            shape((2, span, width), bf16),
            shape((2, span, width), bf16),
            shape((2, span, width), f32),
        ],
        scratch_shapes=[
            pltpu.VMEM((rows, HS), f32),
            pltpu.VMEM((rows, HS), f32),
            pltpu.VMEM((2, 3 * span, rows), bf16),
            pltpu.VMEM((2, 3 * span, rows), bf16),
        ],
        compiler_params=pltpu.CompilerParams(vmem_limit_bytes=VMEM_BYTES),
        cost_estimate=pl.CostEstimate(
            flops=12 * rows * 3 * span * width, bytes_accessed=10 * rows * width, transcendentals=0
        ),
        name="attention",
    )(lists, places, totals, query, cot, gain, key_gain, held, halo_n, halo_a)


def combine_kernel(
    own, from_near, from_across, key, key_gain, inner_query, grad_key, value_grad, inner
):
    total = own[0] + from_near[0].astype(jnp.float32) + from_across[0].astype(jnp.float32)
    grad_key[...] = total
    value_grad[...] = (
        own[1] + from_near[1].astype(jnp.float32) + from_across[1].astype(jnp.float32)
    ).astype(jnp.bfloat16)
    rows = inner_query.shape[1]
    inner[:, :rows] = inner_query[...]
    inner[:, rows:] = across_rows(key[...].astype(jnp.float32) * (total * key_gain[...]))


def combine(own, from_near, from_across, key, key_gain, inner_query):
    _, rows, width = own.shape
    shape = jax.ShapeDtypeStruct
    return pl.pallas_call(
        combine_kernel,
        out_shape=[
            shape((rows, width), jnp.float32),
            shape((rows, width), jnp.bfloat16),
            shape((1, inner_query.shape[1] + rows), jnp.float32),
        ],
        compiler_params=pltpu.CompilerParams(vmem_limit_bytes=VMEM_BYTES),
        name="combine",
    )(own, from_near, from_across, key, key_gain, inner_query)


def norms_backward_kernel(
    totals, inner_parts, gains, query, grad_query, query_gain, key, grad_key, key_gain,
    query_out, key_out, query_gain_grad, key_gain_grad,
):
    rows = query.shape[0]
    inner = inner_parts[0]
    for index in range(1, len(inner_parts)):
        inner = inner + inner_parts[index]
    scale = inverse_rms(totals[...])
    shrink = scale * scale * scale * inner * (1.0 / D)

    def one(start, out, raw, grad, gain):
        here = slice(start, start + BLOCK)
        wide, less = as_columns(scale[:, here]), as_columns(shrink[:, here])
        first = start % rows
        there = slice(first, first + BLOCK)
        for lane in range(0, raw.shape[1], HS):
            lanes = slice(lane, lane + HS)
            out[there, lanes] = (
                wide * (grad[there, lanes] * gain[:, lanes])
                - raw[there, lanes].astype(jnp.float32) * less
            ).astype(jnp.bfloat16)

    for start in range(0, rows, BLOCK):
        one(start, query_out, query, grad_query, query_gain)
    one(rows, key_out, key, grad_key, key_gain)
    query_gain_grad[...] = gains[0]
    key_gain_grad[...] = gains[1]


def norms_backward(totals, inner_parts, gains, *rest):
    query, key = rest[0], rest[3]
    count = len(inner_parts)

    def kernel(totals, *refs):
        parts = [ref[...] for ref in refs[:count]]
        norms_backward_kernel(totals, parts, *refs[count:])

    shape = jax.ShapeDtypeStruct
    width = query.shape[1]
    return pl.pallas_call(
        kernel,
        out_shape=[
            shape(query.shape, jnp.bfloat16),
            shape(key.shape, jnp.bfloat16),
            shape((width,), jnp.float32),
            shape((width,), jnp.float32),
        ],
        compiler_params=pltpu.CompilerParams(vmem_limit_bytes=VMEM_BYTES),
        name="norms_backward",
    )(totals, *inner_parts, gains, *rest)


def swap_near(value):
    return lax.ppermute(value, "core", [(0, 1), (1, 0)])


def swap_across(value):
    size = 1
    for axis in LINE:
        size *= lax.axis_size(axis)
    pairs = []
    for i in range(1, size - 1, 2):
        pairs += [(i, i + 1), (i + 1, i)]
    return lax.ppermute(value, LINE, pairs)


def on_device(video_query, audio_key, audio_value, cotangent, query_gain, key_gain, time_lists):
    place = lax.axis_index(LINE)
    core = lax.axis_index("core")
    video_query, audio_key, audio_value, cotangent = (
        pltpu.with_memory_space_constraint(argument, pltpu.HBM)
        for argument in (video_query, audio_key, audio_value, cotangent)
    )
    places = jnp.stack([place + 1 - 2 * core, place - 1 + 2 * core]).astype(jnp.int32)
    query_gain = query_gain[None]
    key_gain = key_gain[None]
    totals = lax.psum(squares(video_query, audio_key), "tp")
    held = norm_keys(totals, audio_key, audio_value, key_gain)
    halo_a = swap_across(held)
    halo_n = swap_near(held)
    (attended, grad_query, inner_query, gains, to_near, to_across, own) = attention(
        time_lists,
        places,
        totals,
        video_query,
        cotangent,
        query_gain,
        key_gain,
        held,
        halo_n,
        halo_a,
    )
    from_across = swap_across(to_across)
    from_near = swap_near(to_near)
    for axis in ("core", "x", "y"):
        gains = lax.psum(gains, axis)
    grad_key, audio_value_grad, inner = combine(
        own, from_near, from_across, audio_key, key_gain, inner_query
    )
    inner, gains = lax.optimization_barrier((inner, gains))
    size = lax.axis_size("tp")
    inner_parts = [inner] + [
        lax.ppermute(inner, "tp", [(i, (i + by) % size) for i in range(size)])
        for by in range(1, size)
    ]
    gains = lax.psum(gains, "far")
    video_query_grad, audio_key_grad, query_gain_grad, key_gain_grad = norms_backward(
        totals,
        inner_parts,
        gains,
        video_query,
        grad_query,
        query_gain,
        audio_key,
        grad_key,
        key_gain,
    )
    return (
        attended,
        video_query_grad,
        audio_key_grad,
        audio_value_grad,
        query_gain_grad,
        key_gain_grad,
    )


def solution(mesh):
    far = 4
    video, audio, tp = (mesh.shape[name] for name in ("video", "audio", "tp"))
    fine = Mesh(
        np.asarray(mesh.devices).reshape(video // far, far, audio // 2, 2, tp), (*LINE, "tp")
    )
    tokens = P(LINE, "tp")
    per_feature = P("tp")
    return jax.shard_map(
        on_device,
        mesh=fine,
        in_specs=(tokens, tokens, tokens, tokens, per_feature, per_feature, P(LINE, None)),
        out_specs=(tokens, tokens, tokens, tokens, per_feature, per_feature),
        check_vma=False,
    )
```

```python
import numpy as np
import jax
import jax.numpy as jnp
from jax import lax
from jax.experimental import pallas as pl
from jax.experimental.pallas import tpu as pltpu
from jax.sharding import Mesh, PartitionSpec as P

D = 3072
HS = 128
BLOCK = 128
FACTOR = HS ** (-0.5)
LOG2E = 1.4426950408889634
EPSILON = 1e-06
EXCLUDED = -1e30
VMEM_BYTES = 24 * 1024 * 1024
LINE = ("y", "far", "x", "core")


def by_last(left, right):
    return lax.dot_general(
        left, right, (((1,), (1,)), ((), ())), preferred_element_type=jnp.float32
    )


def plain(left, right):
    return jnp.dot(left, right, preferred_element_type=jnp.float32)


def across_rows(values):
    rows, width = values.shape
    total = values[:, :HS]
    for start in range(HS, width, HS):
        total = total + values[:, start : start + HS]
    return jnp.sum(total.T, axis=0, keepdims=True)


def as_columns(row):
    return jnp.broadcast_to(row, (HS, row.shape[1])).T


def inverse_rms(total):
    return lax.rsqrt(total * (1.0 / D) + EPSILON)


def squares_kernel(query, key, totals):
    rows = query.shape[0]
    for start in range(0, rows, BLOCK):
        part = query[start : start + BLOCK].astype(jnp.float32)
        totals[:, start : start + BLOCK] = across_rows(part * part)
    part = key[...].astype(jnp.float32)
    totals[:, rows:] = across_rows(part * part)


def squares(query, key):
    return pl.pallas_call(
        squares_kernel,
        out_shape=jax.ShapeDtypeStruct((1, query.shape[0] + key.shape[0]), jnp.float32),
        compiler_params=pltpu.CompilerParams(vmem_limit_bytes=VMEM_BYTES),
        name="squares",
    )(query, key)


def norm_keys_kernel(totals, key, value, gain, held):
    first = totals.shape[1] - key.shape[0]
    scale = as_columns(inverse_rms(totals[:, first:]))
    for start in range(0, key.shape[1], HS):
        lanes = slice(start, start + HS)
        held[0, :, lanes] = (key[:, lanes].astype(jnp.float32) * scale * gain[lanes][None]).astype(
            jnp.bfloat16
        )
    held[1] = value[...]


def norm_keys(totals, key, value, gain):
    return pl.pallas_call(
        norm_keys_kernel,
        out_shape=jax.ShapeDtypeStruct((2, *key.shape), jnp.bfloat16),
        compiler_params=pltpu.CompilerParams(vmem_limit_bytes=VMEM_BYTES),
        name="norm_keys",
    )(totals, key, value, gain)


def attention_kernel(
    lists, places, totals, query, cot, gain, key_gain, held, halo_n, halo_a,
    attended, grad_query, inner, gains, near, across, own,
    scale_cols, inner_sum, key_sum, probs_low, grad_low,
):
    head = pl.program_id(0)
    rows = query.shape[0]
    span = held.shape[1]

    @pl.when(head == 0)
    def _():
        scale_cols[...] = as_columns(inverse_rms(totals[:, :rows]))
        inner_sum[...] = jnp.zeros_like(inner_sum)
        key_sum[...] = jnp.zeros_like(key_sum)

    def closed(block, place):
        found = lists[block, 0] == place
        for entry in range(1, lists.shape[1]):
            found = jnp.logical_or(found, lists[block, entry] == place)
        return jnp.where(found, 0.0, EXCLUDED)

    def soften(lanes, slot, keys, values, normed, upstream, blocks):
        part = slice(blocks[0] * BLOCK, (blocks[-1] + 1) * BLOCK)
        scores = by_last(keys, normed[part])
        scores = jnp.concatenate(
            [scores[:span] + shut(blocks, 0), scores[span : 2 * span], scores[2 * span :] + shut(blocks, 1)],
            axis=0,
        )
        highest = jnp.max(scores, axis=0, keepdims=True)
        weights = jnp.exp2((scores - highest) * (FACTOR * LOG2E))
        share = 1.0 / jnp.sum(weights, axis=0, keepdims=True)
        probs_low[slot, :, part] = (weights * share).astype(jnp.bfloat16)
        grad_probs = by_last(values, upstream[part])
        delta = jnp.sum(weights * grad_probs, axis=0, keepdims=True) * share
        grad_low[slot, :, part] = (weights * ((grad_probs - delta) * (share * FACTOR))).astype(
            jnp.bfloat16
        )

    def shut(blocks, side):
        if len(blocks) == 1:
            return closed(blocks[0], places[side])
        return jnp.concatenate([jnp.full((1, BLOCK), closed(b, places[side])) for b in blocks], axis=1)

    def prepare(slot):
        lanes = slice(slot * HS, (slot + 1) * HS)
        raw = query[:, lanes].astype(jnp.float32)
        scaled = raw * scale_cols[...]
        normed = (scaled * gain[:, lanes]).astype(jnp.bfloat16)
        keys = jnp.concatenate([halo_n[0, :, lanes], held[0, :, lanes], halo_a[0, :, lanes]], axis=0)
        values = jnp.concatenate([halo_n[1, :, lanes], held[1, :, lanes], halo_a[1, :, lanes]], axis=0)
        return lanes, raw, scaled, normed, values, keys, cot[:, lanes]

    def finish(slot, lanes, raw, scaled, normed, values, keys, upstream):
        low = probs_low[slot]
        grads = grad_low[slot]
        attended[:, lanes] = plain(values.T, low).T.astype(jnp.bfloat16)
        grad = plain(keys.T, grads).T
        grad_query[:, lanes] = grad
        inner_sum[...] += raw * grad * gain[:, lanes]
        grad_keys = plain(grads, normed)
        grad_values = plain(low, upstream)
        gains[0:1, lanes] = jnp.sum(grad * scaled, axis=0, keepdims=True)
        products = grad_keys * keys.astype(jnp.float32)
        key_sum[...] += products
        gains[1:2, lanes] = jnp.sum(products, axis=0, keepdims=True) / key_gain[:, lanes]
        near[0, :, lanes] = grad_keys[:span].astype(jnp.bfloat16)
        near[1, :, lanes] = grad_values[:span].astype(jnp.bfloat16)
        own[0, :, lanes] = grad_keys[span : 2 * span]
        own[1, :, lanes] = grad_values[span : 2 * span]
        across[0, :, lanes] = grad_keys[2 * span :].astype(jnp.bfloat16)
        across[1, :, lanes] = grad_values[2 * span :].astype(jnp.bfloat16)

    total = rows // BLOCK
    groups = [list(range(i, min(i + 2, total))) for i in range(0, total, 2)]
    ready = [prepare(slot) for slot in range(2)]
    for slot in range(2):
        lanes, raw, scaled, normed, values, keys, upstream = ready[slot]
        for blocks in groups:
            soften(lanes, slot, keys, values, normed, upstream, blocks)
        if slot and 1 == 1:
            finish(slot - 1, *ready[slot - 1])
        if 1 == 0:
            finish(slot, *ready[slot])
    if 1 == 1:
        finish(2 - 1, *ready[-1])

    @pl.when(head == pl.num_programs(0) - 1)
    def _():
        inner[:, :rows] = across_rows(inner_sum[...])
        inner[:, rows:] = across_rows(key_sum[...])


def attention(lists, places, totals, query, cot, gain, key_gain, held, halo_n, halo_a):
    rows, width = query.shape
    heads = width // (2 * HS)
    span = held.shape[1]

    def whole(shape):
        return pl.BlockSpec(shape, lambda h: (0,) * len(shape))

    def of_head(*lead):
        return pl.BlockSpec((*lead, 2 * HS), lambda h: (0,) * len(lead) + (h,))

    f32, bf16 = jnp.float32, jnp.bfloat16
    shape = jax.ShapeDtypeStruct
    scalars = pl.BlockSpec(memory_space=pltpu.SMEM)
    return pl.pallas_call(
        attention_kernel,
        grid=(heads,),
        in_specs=[scalars] * 2
        + [whole(totals.shape)]
        + [of_head(rows)] * 2
        + [of_head(1)] * 2
        + [of_head(2, span)] * 3,
        out_specs=[
            of_head(rows),
            of_head(rows),
            whole((1, rows + 3 * span)),
            of_head(2),
            of_head(2, span),
            of_head(2, span),
            of_head(2, span),
        ],
        out_shape=[
            shape((rows, width), bf16),
            shape((rows, width), f32),
            pltpu.HBM((1, rows + 3 * span), f32),
            pltpu.HBM((2, width), f32),
            pltpu.HBM((2, span, width), bf16),
            pltpu.HBM((2, span, width), bf16),
            shape((2, span, width), f32),
        ],
        scratch_shapes=[
            pltpu.VMEM((rows, HS), f32),
            pltpu.VMEM((rows, HS), f32),
            pltpu.VMEM((3 * span, HS), f32),
            pltpu.VMEM((2, 3 * span, rows), bf16),
            pltpu.VMEM((2, 3 * span, rows), bf16),
        ],
        compiler_params=pltpu.CompilerParams(vmem_limit_bytes=VMEM_BYTES),
        cost_estimate=pl.CostEstimate(
            flops=12 * rows * 3 * span * width, bytes_accessed=10 * rows * width, transcendentals=0
        ),
        name="attention",
    )(lists, places, totals, query, cot, gain, key_gain, held, halo_n, halo_a)


def norms_backward_kernel(
    totals, inner, inner_n, inner_a, gains, query, grad_query, query_gain, key, key_gain,
    own, from_near, from_across,
    query_out, key_out, value_out, query_gain_grad, key_gain_grad,
):
    rows = query.shape[0]
    span = key.shape[0]
    scale = inverse_rms(totals[...])
    query_scale, key_scale = scale[:, :rows], scale[:, rows:]
    query_less = query_scale * query_scale * query_scale * inner[:, :rows] * (1.0 / D)
    key_inner = (
        inner_n[:, rows : rows + span]
        + inner[:, rows + span : rows + 2 * span]
        + inner_a[:, rows + 2 * span :]
    )
    key_less = key_scale * key_scale * key_inner * (1.0 / D)

    for start in range(0, rows, BLOCK):
        here = slice(start, start + BLOCK)
        wide, less = as_columns(query_scale[:, here]), as_columns(query_less[:, here])
        for lane in range(0, query.shape[1], HS):
            lanes = slice(lane, lane + HS)
            query_out[here, lanes] = (
                wide * (grad_query[here, lanes] * query_gain[:, lanes])
                - query[here, lanes].astype(jnp.float32) * less
            ).astype(jnp.bfloat16)
    for start in range(0, span, BLOCK):
        here = slice(start, start + BLOCK)
        wide, less = as_columns(key_scale[:, here]), as_columns(key_less[:, here])
        for lane in range(0, key.shape[1], HS):
            lanes = slice(lane, lane + HS)
            grad_key, grad_value = (
                own[lead, here, lanes]
                + from_near[lead, here, lanes].astype(jnp.float32)
                + from_across[lead, here, lanes].astype(jnp.float32)
                for lead in (0, 1)
            )
            key_out[here, lanes] = (
                wide * (grad_key * key_gain[:, lanes]) - key[here, lanes].astype(jnp.float32) * less
            ).astype(jnp.bfloat16)
            value_out[here, lanes] = grad_value.astype(jnp.bfloat16)
    query_gain_grad[...] = gains[0]
    key_gain_grad[...] = gains[1]


def norms_backward(*operands):
    query, key = operands[5], operands[8]
    shape = jax.ShapeDtypeStruct
    width = query.shape[1]
    return pl.pallas_call(
        norms_backward_kernel,
        out_shape=[
            shape(query.shape, jnp.bfloat16),
            shape(key.shape, jnp.bfloat16),
            shape(key.shape, jnp.bfloat16),
            shape((width,), jnp.float32),
            shape((width,), jnp.float32),
        ],
        compiler_params=pltpu.CompilerParams(vmem_limit_bytes=VMEM_BYTES),
        name="norms_backward",
    )(*operands)


def in_hbm(value):
    return pltpu.with_memory_space_constraint(value, pltpu.HBM)


def in_vmem(value):
    return pltpu.with_memory_space_constraint(value, pltpu.VMEM)


def swap_near(value):
    return lax.ppermute(value, "core", [(0, 1), (1, 0)])


def swap_across(value):
    size = 1
    for axis in LINE:
        size *= lax.axis_size(axis)
    pairs = []
    for i in range(1, size - 1, 2):
        pairs += [(i, i + 1), (i + 1, i)]
    return lax.ppermute(value, LINE, pairs)


def on_device(video_query, audio_key, audio_value, cotangent, query_gain, key_gain, time_lists):
    place = lax.axis_index(LINE)
    core = lax.axis_index("core")
    video_query, audio_key, audio_value, cotangent = (
        in_hbm(argument)
        for argument in (video_query, audio_key, audio_value, cotangent)
    )
    places = jnp.stack([place + 1 - 2 * core, place - 1 + 2 * core]).astype(jnp.int32)
    totals = lax.psum(squares(video_query, audio_key), "tp")
    held = norm_keys(totals, audio_key, audio_value, in_hbm(key_gain))
    query_gain = query_gain[None]
    key_gain = key_gain[None]
    halo_a = in_vmem(swap_across(held))
    halo_n = in_vmem(swap_near(held))
    attended, grad_query, inner, gains, to_near, to_across, own = attention(
        time_lists,
        places,
        totals,
        video_query,
        cotangent,
        query_gain,
        key_gain,
        held,
        halo_n,
        halo_a,
    )
    inner = lax.psum(inner, "tp")
    inner, gains = lax.optimization_barrier((inner, gains))
    inner_a = swap_across(inner)
    inner_n = swap_near(inner)
    gains = lax.psum(gains, "core")
    inner_a, inner_n, gains, to_near, to_across = lax.optimization_barrier(
        (inner_a, inner_n, gains, to_near, to_across)
    )
    from_across = in_vmem(swap_across(to_across))
    from_near = in_vmem(swap_near(to_near))
    for axis in ("x", "y", "far"):
        gains = lax.psum(gains, axis)
    video_query_grad, audio_key_grad, audio_value_grad, query_gain_grad, key_gain_grad = (
        norms_backward(
            totals,
            inner,
            inner_n,
            inner_a,
            gains,
            video_query,
            grad_query,
            query_gain,
            audio_key,
            key_gain,
            own,
            from_near,
            from_across,
        )
    )
    return (
        attended,
        video_query_grad,
        audio_key_grad,
        audio_value_grad,
        query_gain_grad,
        key_gain_grad,
    )


def solution(mesh):
    far = 4
    video, audio, tp = (mesh.shape[name] for name in ("video", "audio", "tp"))
    fine = Mesh(
        np.asarray(mesh.devices).reshape(video // far, far, audio // 2, 2, tp), (*LINE, "tp")
    )
    tokens = P(LINE, "tp")
    per_feature = P("tp")
    return jax.shard_map(
        on_device,
        mesh=fine,
        in_specs=(tokens, tokens, tokens, tokens, per_feature, per_feature, P(LINE, None)),
        out_specs=(tokens, tokens, tokens, tokens, per_feature, per_feature),
        check_vma=False,
    )
```

```python
import numpy as np
import jax
import jax.numpy as jnp
from jax import lax
from jax.experimental import pallas as pl
from jax.experimental.pallas import tpu as pltpu
from jax.sharding import Mesh, PartitionSpec as P

D = 3072
HS = 128
BLOCK = 128
FACTOR = HS ** (-0.5)
LOG2E = 1.4426950408889634
EPSILON = 1e-06
EXCLUDED = -1e30
VMEM_BYTES = 24 * 1024 * 1024
LINE = ("y", "far", "x", "core")


def by_last(left, right):
    return lax.dot_general(
        left, right, (((1,), (1,)), ((), ())), preferred_element_type=jnp.float32
    )


def plain(left, right):
    return jnp.dot(left, right, preferred_element_type=jnp.float32)


def across_rows(values):
    rows, width = values.shape
    total = values[:, :HS]
    for start in range(HS, width, HS):
        total = total + values[:, start : start + HS]
    return jnp.sum(total.T, axis=0, keepdims=True)


def as_columns(row):
    return jnp.broadcast_to(row, (HS, row.shape[1])).T


def inverse_rms(total):
    return lax.rsqrt(total * (1.0 / D) + EPSILON)


def squares_kernel(query, key, totals):
    rows = query.shape[0]
    for start in range(0, rows, BLOCK):
        part = query[start : start + BLOCK].astype(jnp.float32)
        totals[:, start : start + BLOCK] = across_rows(part * part)
    part = key[...].astype(jnp.float32)
    totals[:, rows:] = across_rows(part * part)


def squares(query, key):
    return pl.pallas_call(
        squares_kernel,
        out_shape=jax.ShapeDtypeStruct((1, query.shape[0] + key.shape[0]), jnp.float32),
        compiler_params=pltpu.CompilerParams(vmem_limit_bytes=VMEM_BYTES),
        name="squares",
    )(query, key)


def norm_keys_kernel(totals, key, value, gain, held):
    first = totals.shape[1] - key.shape[0]
    scale = as_columns(inverse_rms(totals[:, first:]))
    for start in range(0, key.shape[1], HS):
        lanes = slice(start, start + HS)
        held[0, :, lanes] = (key[:, lanes].astype(jnp.float32) * scale * gain[lanes][None]).astype(
            jnp.bfloat16
        )
    held[1] = value[...]


def norm_keys(totals, key, value, gain):
    return pl.pallas_call(
        norm_keys_kernel,
        out_shape=jax.ShapeDtypeStruct((2, *key.shape), jnp.bfloat16),
        compiler_params=pltpu.CompilerParams(vmem_limit_bytes=VMEM_BYTES),
        name="norm_keys",
    )(totals, key, value, gain)


def attention_kernel(
    lists, places, totals, query, cot, gain, key_gain, held, halo_n, halo_a,
    attended, grad_query, inner, gains, near, across_k, across_v, own_k, own_v,
    scale_cols, inner_sum, probs_low, grad_low,
):
    head = pl.program_id(0)
    rows = query.shape[0]
    span = held.shape[1]

    @pl.when(head == 0)
    def _():
        scale_cols[...] = as_columns(inverse_rms(totals[:, :rows]))
        inner_sum[...] = jnp.zeros_like(inner_sum)

    def closed(block, place):
        found = lists[block, 0] == place
        for entry in range(1, lists.shape[1]):
            found = jnp.logical_or(found, lists[block, entry] == place)
        return jnp.where(found, 0.0, EXCLUDED)

    def soften(lanes, slot, keys, values, normed, upstream, blocks):
        part = slice(blocks[0] * BLOCK, (blocks[-1] + 1) * BLOCK)
        scores = by_last(keys, normed[part])
        scores = jnp.concatenate(
            [scores[:span] + shut(blocks, 0), scores[span : 2 * span], scores[2 * span :] + shut(blocks, 1)],
            axis=0,
        )
        highest = jnp.max(scores, axis=0, keepdims=True)
        weights = jnp.exp2((scores - highest) * (FACTOR * LOG2E))
        share = 1.0 / jnp.sum(weights, axis=0, keepdims=True)
        probs_low[slot, :, part] = (weights * share).astype(jnp.bfloat16)
        grad_probs = by_last(values, upstream[part])
        delta = jnp.sum(weights * grad_probs, axis=0, keepdims=True) * share
        grad_low[slot, :, part] = (weights * ((grad_probs - delta) * (share * FACTOR))).astype(
            jnp.bfloat16
        )

    def shut(blocks, side):
        if len(blocks) == 1:
            return closed(blocks[0], places[side])
        return jnp.concatenate([jnp.full((1, BLOCK), closed(b, places[side])) for b in blocks], axis=1)

    def prepare(slot):
        lanes = slice(slot * HS, (slot + 1) * HS)
        raw = query[:, lanes].astype(jnp.float32)
        scaled = raw * scale_cols[...]
        normed = (scaled * gain[:, lanes]).astype(jnp.bfloat16)
        keys = jnp.concatenate([halo_n[0, :, lanes], held[0, :, lanes], halo_a[0, :, lanes]], axis=0)
        values = jnp.concatenate([halo_n[1, :, lanes], held[1, :, lanes], halo_a[1, :, lanes]], axis=0)
        return lanes, raw, scaled, normed, values, keys, cot[:, lanes]

    def finish(slot, lanes, raw, scaled, normed, values, keys, upstream):
        low = probs_low[slot]
        grads = grad_low[slot]
        attended[:, lanes] = plain(values.T, low).T.astype(jnp.bfloat16)
        grad = plain(keys.T, grads).T
        grad_query[:, lanes] = grad
        inner_sum[...] += raw * grad * gain[:, lanes]
        grad_keys = plain(grads, normed)
        grad_values = plain(low, upstream)
        gains[0:1, lanes] = jnp.sum(grad * scaled, axis=0, keepdims=True)
        gains[1:2, lanes] = (
            jnp.sum(grad_keys * keys.astype(jnp.float32), axis=0, keepdims=True)
            / key_gain[:, lanes]
        )
        near[0, :, lanes] = grad_keys[:span].astype(jnp.bfloat16)
        near[1, :, lanes] = grad_values[:span].astype(jnp.bfloat16)
        own_k[:, lanes] = grad_keys[span : 2 * span]
        own_v[:, lanes] = grad_values[span : 2 * span]
        across_k[:, lanes] = grad_keys[2 * span :].astype(jnp.bfloat16)
        across_v[:, lanes] = grad_values[2 * span :].astype(jnp.bfloat16)

    total = rows // BLOCK
    groups = [list(range(i, min(i + 2, total))) for i in range(0, total, 2)]
    ready = [prepare(slot) for slot in range(2)]
    for slot in range(2):
        lanes, raw, scaled, normed, values, keys, upstream = ready[slot]
        for blocks in groups:
            soften(lanes, slot, keys, values, normed, upstream, blocks)
        if slot and 1 == 1:
            finish(slot - 1, *ready[slot - 1])
        if 1 == 0:
            finish(slot, *ready[slot])
    if 1 == 1:
        finish(2 - 1, *ready[-1])

    @pl.when(head == pl.num_programs(0) - 1)
    def _():
        inner[...] = across_rows(inner_sum[...])


def attention(lists, places, totals, query, cot, gain, key_gain, held, halo_n, halo_a):
    rows, width = query.shape
    heads = width // (2 * HS)
    span = held.shape[1]

    def whole(shape):
        return pl.BlockSpec(shape, lambda h: (0,) * len(shape))

    def of_head(*lead):
        return pl.BlockSpec((*lead, 2 * HS), lambda h: (0,) * len(lead) + (h,))

    f32, bf16 = jnp.float32, jnp.bfloat16
    shape = jax.ShapeDtypeStruct
    scalars = pl.BlockSpec(memory_space=pltpu.SMEM)
    return pl.pallas_call(
        attention_kernel,
        grid=(heads,),
        in_specs=[scalars] * 2
        + [whole(totals.shape)]
        + [of_head(rows)] * 2
        + [of_head(1)] * 2
        + [of_head(2, span)] * 3,
        out_specs=[
            of_head(rows),
            of_head(rows),
            whole((1, rows)),
            of_head(2),
            of_head(2, span),
            of_head(span),
            of_head(span),
            of_head(span),
            of_head(span),
        ],
        out_shape=[
            shape((rows, width), bf16),
            shape((rows, width), f32),
            pltpu.HBM((1, rows), f32),
            pltpu.HBM((2, width), f32),
            pltpu.HBM((2, span, width), bf16),
            pltpu.HBM((span, width), bf16),
            pltpu.HBM((span, width), bf16),
            shape((span, width), f32),
            shape((span, width), f32),
        ],
        scratch_shapes=[
            pltpu.VMEM((rows, HS), f32),
            pltpu.VMEM((rows, HS), f32),
            pltpu.VMEM((2, 3 * span, rows), bf16),
            pltpu.VMEM((2, 3 * span, rows), bf16),
        ],
        compiler_params=pltpu.CompilerParams(vmem_limit_bytes=VMEM_BYTES),
        cost_estimate=pl.CostEstimate(
            flops=12 * rows * 3 * span * width, bytes_accessed=10 * rows * width, transcendentals=0
        ),
        name="attention",
    )(lists, places, totals, query, cot, gain, key_gain, held, halo_n, halo_a)


def combine_kernel(own, from_near, from_across, key, key_gain, inner_query, grad_key, inner):
    total = own[...] + from_near[0].astype(jnp.float32) + from_across[...].astype(jnp.float32)
    grad_key[...] = total
    rows = inner_query.shape[1]
    inner[:, :rows] = inner_query[...]
    inner[:, rows:] = across_rows(key[...].astype(jnp.float32) * (total * key_gain[...]))


def combine(own, from_near, from_across, key, key_gain, inner_query):
    shape = jax.ShapeDtypeStruct
    rows, width = own.shape
    whole = pl.BlockSpec(memory_space=pltpu.VMEM)
    first = pl.BlockSpec((1, rows, width), lambda i: (0, 0, 0))
    return pl.pallas_call(
        combine_kernel,
        grid=(1,),
        in_specs=[whole, first] + [whole] * 4,
        out_specs=[whole, whole],
        out_shape=[
            shape((rows, width), jnp.float32),
            shape((1, inner_query.shape[1] + rows), jnp.float32),
        ],
        compiler_params=pltpu.CompilerParams(vmem_limit_bytes=VMEM_BYTES),
        name="combine",
    )(own, from_near, from_across, key, key_gain, inner_query)


def norms_backward_kernel(
    totals, inner_parts, gains, query, grad_query, query_gain, key, grad_key, key_gain,
    own, from_near, from_across,
    query_out, key_out, value_out, query_gain_grad, key_gain_grad,
):
    rows = query.shape[0]
    inner = inner_parts[0]
    for index in range(1, len(inner_parts)):
        inner = inner + inner_parts[index]
    scale = inverse_rms(totals[...])
    shrink = scale * scale * scale * inner * (1.0 / D)

    def one(start, out, raw, grad, gain):
        here = slice(start, start + BLOCK)
        wide, less = as_columns(scale[:, here]), as_columns(shrink[:, here])
        first = start % rows
        there = slice(first, first + BLOCK)
        for lane in range(0, raw.shape[1], HS):
            lanes = slice(lane, lane + HS)
            out[there, lanes] = (
                wide * (grad[there, lanes] * gain[:, lanes])
                - raw[there, lanes].astype(jnp.float32) * less
            ).astype(jnp.bfloat16)

    for start in range(0, rows, BLOCK):
        one(start, query_out, query, grad_query, query_gain)
    one(rows, key_out, key, grad_key, key_gain)
    value_out[...] = (
        own[...] + from_near[0].astype(jnp.float32) + from_across[...].astype(jnp.float32)
    ).astype(jnp.bfloat16)
    query_gain_grad[...] = gains[0]
    key_gain_grad[...] = gains[1]


def norms_backward(totals, inner_parts, gains, *rest):
    query, key = rest[0], rest[3]
    count = len(inner_parts)

    def kernel(totals, *refs):
        parts = [ref[...] for ref in refs[:count]]
        norms_backward_kernel(totals, parts, *refs[count:])

    shape = jax.ShapeDtypeStruct
    width = query.shape[1]
    whole = pl.BlockSpec(memory_space=pltpu.VMEM)
    second = pl.BlockSpec((1, *key.shape), lambda i: (1, 0, 0))
    return pl.pallas_call(
        kernel,
        grid=(1,),
        in_specs=[whole] * (count + 9) + [second, whole],
        out_specs=[whole] * 5,
        out_shape=[
            shape(query.shape, jnp.bfloat16),
            shape(key.shape, jnp.bfloat16),
            shape(key.shape, jnp.bfloat16),
            shape((width,), jnp.float32),
            shape((width,), jnp.float32),
        ],
        compiler_params=pltpu.CompilerParams(vmem_limit_bytes=VMEM_BYTES),
        name="norms_backward",
    )(totals, *inner_parts, gains, *rest)


def in_hbm(value):
    return pltpu.with_memory_space_constraint(value, pltpu.HBM)


def swap_near(value):
    return lax.ppermute(value, "core", [(0, 1), (1, 0)])


def swap_across(value):
    size = 1
    for axis in LINE:
        size *= lax.axis_size(axis)
    pairs = []
    for i in range(1, size - 1, 2):
        pairs += [(i, i + 1), (i + 1, i)]
    return lax.ppermute(value, LINE, pairs)


def on_device(video_query, audio_key, audio_value, cotangent, query_gain, key_gain, time_lists):
    place = lax.axis_index(LINE)
    core = lax.axis_index("core")
    video_query, audio_key, audio_value, cotangent = (
        in_hbm(argument)
        for argument in (video_query, audio_key, audio_value, cotangent)
    )
    places = jnp.stack([place + 1 - 2 * core, place - 1 + 2 * core]).astype(jnp.int32)
    totals = lax.psum(squares(video_query, audio_key), "tp")
    held = norm_keys(totals, audio_key, audio_value, in_hbm(key_gain))
    query_gain = query_gain[None]
    key_gain = key_gain[None]
    halo_a = in_hbm(swap_across(held))
    halo_n = in_hbm(swap_near(held))
    (
        attended, grad_query, inner_query, gains, to_near, to_across_k, to_across_v, own_k, own_v
    ) = attention(
        time_lists,
        places,
        totals,
        video_query,
        cotangent,
        query_gain,
        key_gain,
        held,
        halo_n,
        halo_a,
    )
    from_across_k = swap_across(to_across_k)
    from_near = swap_near(to_near)
    for axis in ("core", "x"):
        gains = lax.psum(gains, axis)
    gains, to_across_v = lax.optimization_barrier((gains, to_across_v))
    from_across_v = swap_across(to_across_v)
    gains = lax.psum(gains, "y")
    grad_key, inner = combine(
        own_k, from_near, in_hbm(from_across_k), audio_key, key_gain, in_hbm(inner_query)
    )
    inner, gains = lax.optimization_barrier((inner, gains))
    size = lax.axis_size("tp")
    inner_parts = [inner] + [
        lax.ppermute(inner, "tp", [(i, (i + by) % size) for i in range(size)])
        for by in range(1, size)
    ]
    gains = lax.psum(gains, "far")
    video_query_grad, audio_key_grad, audio_value_grad, query_gain_grad, key_gain_grad = (
        norms_backward(
            totals,
            inner_parts,
            gains,
            video_query,
            grad_query,
            query_gain,
            audio_key,
            grad_key,
            key_gain,
            own_v,
            from_near,
            from_across_v,
        )
    )
    return (
        attended,
        video_query_grad,
        audio_key_grad,
        audio_value_grad,
        query_gain_grad,
        key_gain_grad,
    )


def solution(mesh):
    far = 4
    video, audio, tp = (mesh.shape[name] for name in ("video", "audio", "tp"))
    fine = Mesh(
        np.asarray(mesh.devices).reshape(video // far, far, audio // 2, 2, tp), (*LINE, "tp")
    )
    tokens = P(LINE, "tp")
    per_feature = P("tp")
    return jax.shard_map(
        on_device,
        mesh=fine,
        in_specs=(tokens, tokens, tokens, tokens, per_feature, per_feature, P(LINE, None)),
        out_specs=(tokens, tokens, tokens, tokens, per_feature, per_feature),
        check_vma=False,
    )
```

```python
import numpy as np
import jax
import jax.numpy as jnp
from jax import lax
from jax.experimental import pallas as pl
from jax.experimental.pallas import tpu as pltpu
from jax.sharding import Mesh, PartitionSpec as P

D = 3072
HS = 128
BLOCK = 128
FACTOR = HS ** (-0.5)
LOG2E = 1.4426950408889634
EPSILON = 1e-06
EXCLUDED = -1e30
VMEM_BYTES = 24 * 1024 * 1024
LINE = ("y", "far", "x", "core")


def by_last(left, right):
    return lax.dot_general(
        left, right, (((1,), (1,)), ((), ())), preferred_element_type=jnp.float32
    )


def plain(left, right):
    return jnp.dot(left, right, preferred_element_type=jnp.float32)


def across_rows(values):
    rows, width = values.shape
    total = values[:, :HS]
    for start in range(HS, width, HS):
        total = total + values[:, start : start + HS]
    return jnp.sum(total.T, axis=0, keepdims=True)


def as_columns(row):
    return jnp.broadcast_to(row, (HS, row.shape[1])).T


def inverse_rms(total):
    return lax.rsqrt(total * (1.0 / D) + EPSILON)


def squares_kernel(query, key, totals):
    rows = query.shape[0]
    for start in range(0, rows, BLOCK):
        part = query[start : start + BLOCK].astype(jnp.float32)
        totals[:, start : start + BLOCK] = across_rows(part * part)
    part = key[...].astype(jnp.float32)
    totals[:, rows:] = across_rows(part * part)


def squares(query, key):
    return pl.pallas_call(
        squares_kernel,
        out_shape=jax.ShapeDtypeStruct((1, query.shape[0] + key.shape[0]), jnp.float32),
        compiler_params=pltpu.CompilerParams(vmem_limit_bytes=VMEM_BYTES),
        name="squares",
    )(query, key)


def norm_keys_kernel(totals, key, value, gain, held):
    first = totals.shape[1] - key.shape[0]
    scale = as_columns(inverse_rms(totals[:, first:]))
    for start in range(0, key.shape[1], HS):
        lanes = slice(start, start + HS)
        held[0, :, lanes] = (key[:, lanes].astype(jnp.float32) * scale * gain[lanes][None]).astype(
            jnp.bfloat16
        )
    held[1] = value[...]


def norm_keys(totals, key, value, gain):
    return pl.pallas_call(
        norm_keys_kernel,
        out_shape=jax.ShapeDtypeStruct((2, *key.shape), jnp.bfloat16),
        compiler_params=pltpu.CompilerParams(vmem_limit_bytes=VMEM_BYTES),
        name="norm_keys",
    )(totals, key, value, gain)


def attention_kernel(
    lists, places, totals, query, cot, gain, key_gain, held, halo_n, halo_a,
    attended, grad_query, inner, gains, near, across_k, across_v, own_k, own_v,
    scale_cols, inner_sum, probs_low, grad_low,
):
    head = pl.program_id(0)
    rows = query.shape[0]
    span = held.shape[1]

    @pl.when(head == 0)
    def _():
        scale_cols[...] = as_columns(inverse_rms(totals[:, :rows]))
        inner_sum[...] = jnp.zeros_like(inner_sum)

    def closed(block, place):
        found = lists[block, 0] == place
        for entry in range(1, lists.shape[1]):
            found = jnp.logical_or(found, lists[block, entry] == place)
        return jnp.where(found, 0.0, EXCLUDED)

    def soften(lanes, slot, keys, values, normed, upstream, blocks):
        part = slice(blocks[0] * BLOCK, (blocks[-1] + 1) * BLOCK)
        scores = by_last(keys, normed[part])
        scores = jnp.concatenate(
            [scores[:span] + shut(blocks, 0), scores[span : 2 * span], scores[2 * span :] + shut(blocks, 1)],
            axis=0,
        )
        highest = jnp.max(scores, axis=0, keepdims=True)
        weights = jnp.exp2((scores - highest) * (FACTOR * LOG2E))
        share = 1.0 / jnp.sum(weights, axis=0, keepdims=True)
        probs_low[slot, :, part] = (weights * share).astype(jnp.bfloat16)
        grad_probs = by_last(values, upstream[part])
        delta = jnp.sum(weights * grad_probs, axis=0, keepdims=True) * share
        grad_low[slot, :, part] = (weights * ((grad_probs - delta) * (share * FACTOR))).astype(
            jnp.bfloat16
        )

    def shut(blocks, side):
        if len(blocks) == 1:
            return closed(blocks[0], places[side])
        return jnp.concatenate([jnp.full((1, BLOCK), closed(b, places[side])) for b in blocks], axis=1)

    def prepare(slot):
        lanes = slice(slot * HS, (slot + 1) * HS)
        raw = query[:, lanes].astype(jnp.float32)
        scaled = raw * scale_cols[...]
        normed = (scaled * gain[:, lanes]).astype(jnp.bfloat16)
        keys = jnp.concatenate([halo_n[0, :, lanes], held[0, :, lanes], halo_a[0, :, lanes]], axis=0)
        values = jnp.concatenate([halo_n[1, :, lanes], held[1, :, lanes], halo_a[1, :, lanes]], axis=0)
        return lanes, raw, scaled, normed, values, keys, cot[:, lanes]

    def finish(slot, lanes, raw, scaled, normed, values, keys, upstream):
        low = probs_low[slot]
        grads = grad_low[slot]
        attended[:, lanes] = plain(values.T, low).T.astype(jnp.bfloat16)
        grad = plain(keys.T, grads).T
        grad_query[:, lanes] = grad
        inner_sum[...] += raw * grad * gain[:, lanes]
        grad_keys = plain(grads, normed)
        grad_values = plain(low, upstream)
        gains[0:1, lanes] = jnp.sum(grad * scaled, axis=0, keepdims=True)
        gains[1:2, lanes] = (
            jnp.sum(grad_keys * keys.astype(jnp.float32), axis=0, keepdims=True)
            / key_gain[:, lanes]
        )
        near[0, :, lanes] = grad_keys[:span].astype(jnp.bfloat16)
        near[1, :, lanes] = grad_values[:span].astype(jnp.bfloat16)
        own_k[:, lanes] = grad_keys[span : 2 * span]
        own_v[:, lanes] = grad_values[span : 2 * span]
        across_k[:, lanes] = grad_keys[2 * span :].astype(jnp.bfloat16)
        across_v[:, lanes] = grad_values[2 * span :].astype(jnp.bfloat16)

    total = rows // BLOCK
    groups = [list(range(i, min(i + 2, total))) for i in range(0, total, 2)]
    ready = [prepare(slot) for slot in range(2)]
    for slot in range(2):
        lanes, raw, scaled, normed, values, keys, upstream = ready[slot]
        for blocks in groups:
            soften(lanes, slot, keys, values, normed, upstream, blocks)
        if slot and 1 == 1:
            finish(slot - 1, *ready[slot - 1])
        if 1 == 0:
            finish(slot, *ready[slot])
    if 1 == 1:
        finish(2 - 1, *ready[-1])

    @pl.when(head == pl.num_programs(0) - 1)
    def _():
        inner[...] = across_rows(inner_sum[...])


def attention(lists, places, totals, query, cot, gain, key_gain, held, halo_n, halo_a):
    rows, width = query.shape
    heads = width // (2 * HS)
    span = held.shape[1]

    def whole(shape):
        return pl.BlockSpec(shape, lambda h: (0,) * len(shape))

    def of_head(*lead):
        return pl.BlockSpec((*lead, 2 * HS), lambda h: (0,) * len(lead) + (h,))

    f32, bf16 = jnp.float32, jnp.bfloat16
    shape = jax.ShapeDtypeStruct
    scalars = pl.BlockSpec(memory_space=pltpu.SMEM)
    return pl.pallas_call(
        attention_kernel,
        grid=(heads,),
        in_specs=[scalars] * 2
        + [whole(totals.shape)]
        + [of_head(rows)] * 2
        + [of_head(1)] * 2
        + [of_head(2, span)] * 3,
        out_specs=[
            of_head(rows),
            of_head(rows),
            whole((1, rows)),
            of_head(2),
            of_head(2, span),
            of_head(span),
            of_head(span),
            of_head(span),
            of_head(span),
        ],
        out_shape=[
            shape((rows, width), bf16),
            shape((rows, width), f32),
            pltpu.HBM((1, rows), f32),
            pltpu.HBM((2, width), f32),
            pltpu.HBM((2, span, width), bf16),
            pltpu.HBM((span, width), bf16),
            pltpu.HBM((span, width), bf16),
            shape((span, width), f32),
            shape((span, width), f32),
        ],
        scratch_shapes=[
            pltpu.VMEM((rows, HS), f32),
            pltpu.VMEM((rows, HS), f32),
            pltpu.VMEM((2, 3 * span, rows), bf16),
            pltpu.VMEM((2, 3 * span, rows), bf16),
        ],
        compiler_params=pltpu.CompilerParams(vmem_limit_bytes=VMEM_BYTES),
        cost_estimate=pl.CostEstimate(
            flops=12 * rows * 3 * span * width, bytes_accessed=10 * rows * width, transcendentals=0
        ),
        name="attention",
    )(lists, places, totals, query, cot, gain, key_gain, held, halo_n, halo_a)


def combine_kernel(own, from_near, from_across, key, key_gain, inner_query, grad_key, inner):
    total = own[...] + from_near[0].astype(jnp.float32) + from_across[...].astype(jnp.float32)
    grad_key[...] = total
    rows = inner_query.shape[1]
    inner[:, :rows] = inner_query[...]
    inner[:, rows:] = across_rows(key[...].astype(jnp.float32) * (total * key_gain[...]))


def combine(own, from_near, from_across, key, key_gain, inner_query):
    shape = jax.ShapeDtypeStruct
    rows, width = own.shape
    whole = pl.BlockSpec(memory_space=pltpu.VMEM)
    first = pl.BlockSpec((1, rows, width), lambda i: (0, 0, 0))
    return pl.pallas_call(
        combine_kernel,
        grid=(1,),
        in_specs=[whole, first] + [whole] * 4,
        out_specs=[whole, whole],
        out_shape=[
            shape((rows, width), jnp.float32),
            shape((1, inner_query.shape[1] + rows), jnp.float32),
        ],
        compiler_params=pltpu.CompilerParams(vmem_limit_bytes=VMEM_BYTES),
        name="combine",
    )(own, from_near, from_across, key, key_gain, inner_query)


def norms_backward_kernel(
    totals, inner_parts, gains, query, grad_query, query_gain, key, grad_key, key_gain,
    own, from_near, from_across,
    query_out, key_out, value_out, query_gain_grad, key_gain_grad,
):
    rows = query.shape[0]
    inner = inner_parts[0]
    for index in range(1, len(inner_parts)):
        inner = inner + inner_parts[index]
    scale = inverse_rms(totals[...])
    shrink = scale * scale * scale * inner * (1.0 / D)

    def one(start, out, raw, grad, gain):
        here = slice(start, start + BLOCK)
        wide, less = as_columns(scale[:, here]), as_columns(shrink[:, here])
        first = start % rows
        there = slice(first, first + BLOCK)
        for lane in range(0, raw.shape[1], HS):
            lanes = slice(lane, lane + HS)
            out[there, lanes] = (
                wide * (grad[there, lanes] * gain[:, lanes])
                - raw[there, lanes].astype(jnp.float32) * less
            ).astype(jnp.bfloat16)

    for start in range(0, rows, BLOCK):
        one(start, query_out, query, grad_query, query_gain)
    one(rows, key_out, key, grad_key, key_gain)
    value_out[...] = (
        own[...] + from_near[0].astype(jnp.float32) + from_across[...].astype(jnp.float32)
    ).astype(jnp.bfloat16)
    query_gain_grad[...] = gains[0]
    key_gain_grad[...] = gains[1]


def norms_backward(totals, inner_parts, gains, *rest):
    query, key = rest[0], rest[3]
    count = len(inner_parts)

    def kernel(totals, *refs):
        parts = [ref[...] for ref in refs[:count]]
        norms_backward_kernel(totals, parts, *refs[count:])

    shape = jax.ShapeDtypeStruct
    width = query.shape[1]
    whole = pl.BlockSpec(memory_space=pltpu.VMEM)
    second = pl.BlockSpec((1, *key.shape), lambda i: (1, 0, 0))
    return pl.pallas_call(
        kernel,
        grid=(1,),
        in_specs=[whole] * (count + 9) + [second, whole],
        out_specs=[whole] * 5,
        out_shape=[
            shape(query.shape, jnp.bfloat16),
            shape(key.shape, jnp.bfloat16),
            shape(key.shape, jnp.bfloat16),
            shape((width,), jnp.float32),
            shape((width,), jnp.float32),
        ],
        compiler_params=pltpu.CompilerParams(vmem_limit_bytes=VMEM_BYTES),
        name="norms_backward",
    )(totals, *inner_parts, gains, *rest)


def in_hbm(value):
    return pltpu.with_memory_space_constraint(value, pltpu.HBM)


def swap_near(value):
    return lax.ppermute(value, "core", [(0, 1), (1, 0)])


def swap_across(value):
    size = 1
    for axis in LINE:
        size *= lax.axis_size(axis)
    pairs = []
    for i in range(1, size - 1, 2):
        pairs += [(i, i + 1), (i + 1, i)]
    return lax.ppermute(value, LINE, pairs)


def on_device(video_query, audio_key, audio_value, cotangent, query_gain, key_gain, time_lists):
    place = lax.axis_index(LINE)
    core = lax.axis_index("core")
    video_query, audio_key, audio_value, cotangent = (
        in_hbm(argument)
        for argument in (video_query, audio_key, audio_value, cotangent)
    )
    places = jnp.stack([place + 1 - 2 * core, place - 1 + 2 * core]).astype(jnp.int32)
    totals = lax.psum(squares(video_query, audio_key), "tp")
    held = norm_keys(totals, audio_key, audio_value, in_hbm(key_gain))
    query_gain = query_gain[None]
    key_gain = key_gain[None]
    halo_a = in_hbm(swap_across(held))
    halo_n = in_hbm(swap_near(held))
    (
        attended, grad_query, inner_query, gains, to_near, to_across_k, to_across_v, own_k, own_v
    ) = attention(
        time_lists,
        places,
        totals,
        video_query,
        cotangent,
        query_gain,
        key_gain,
        held,
        halo_n,
        halo_a,
    )
    from_near = swap_near(to_near)
    for axis in ("core", "x"):
        gains = lax.psum(gains, axis)
    gains, to_across_k = lax.optimization_barrier((gains, to_across_k))
    from_across_k = swap_across(to_across_k)
    gains = lax.psum(gains, "y")
    gains, to_across_v = lax.optimization_barrier((gains, to_across_v))
    from_across_v = swap_across(to_across_v)
    grad_key, inner = combine(
        own_k, from_near, in_hbm(from_across_k), audio_key, key_gain, in_hbm(inner_query)
    )
    inner, gains = lax.optimization_barrier((inner, gains))
    size = lax.axis_size("tp")
    inner_parts = [inner] + [
        lax.ppermute(inner, "tp", [(i, (i + by) % size) for i in range(size)])
        for by in range(1, size)
    ]
    gains = lax.psum(gains, "far")
    video_query_grad, audio_key_grad, audio_value_grad, query_gain_grad, key_gain_grad = (
        norms_backward(
            totals,
            inner_parts,
            gains,
            video_query,
            grad_query,
            query_gain,
            audio_key,
            grad_key,
            key_gain,
            own_v,
            from_near,
            from_across_v,
        )
    )
    return (
        attended,
        video_query_grad,
        audio_key_grad,
        audio_value_grad,
        query_gain_grad,
        key_gain_grad,
    )


def solution(mesh):
    far = 4
    video, audio, tp = (mesh.shape[name] for name in ("video", "audio", "tp"))
    fine = Mesh(
        np.asarray(mesh.devices).reshape(video // far, far, audio // 2, 2, tp), (*LINE, "tp")
    )
    tokens = P(LINE, "tp")
    per_feature = P("tp")
    return jax.shard_map(
        on_device,
        mesh=fine,
        in_specs=(tokens, tokens, tokens, tokens, per_feature, per_feature, P(LINE, None)),
        out_specs=(tokens, tokens, tokens, tokens, per_feature, per_feature),
        check_vma=False,
    )
```

```python
import numpy as np
import jax
import jax.numpy as jnp
from jax import lax
from jax.experimental import pallas as pl
from jax.experimental.pallas import tpu as pltpu
from jax.sharding import Mesh, PartitionSpec as P

D = 3072
HS = 128
BLOCK = 128
FACTOR = HS ** (-0.5)
LOG2E = 1.4426950408889634
EPSILON = 1e-06
EXCLUDED = -1e30
VMEM_BYTES = 24 * 1024 * 1024
LINE = ("y", "far", "x", "core")


def by_last(left, right):
    return lax.dot_general(
        left, right, (((1,), (1,)), ((), ())), preferred_element_type=jnp.float32
    )


def plain(left, right):
    return jnp.dot(left, right, preferred_element_type=jnp.float32)


def across_rows(values):
    rows, width = values.shape
    total = values[:, :HS]
    for start in range(HS, width, HS):
        total = total + values[:, start : start + HS]
    return jnp.sum(total.T, axis=0, keepdims=True)


def as_columns(row):
    return jnp.broadcast_to(row, (HS, row.shape[1])).T


def inverse_rms(total):
    return lax.rsqrt(total * (1.0 / D) + EPSILON)


def squares_kernel(query, key, totals):
    rows = query.shape[0]
    for start in range(0, rows, BLOCK):
        part = query[start : start + BLOCK].astype(jnp.float32)
        totals[:, start : start + BLOCK] = across_rows(part * part)
    part = key[...].astype(jnp.float32)
    totals[:, rows:] = across_rows(part * part)


def squares(query, key):
    return pl.pallas_call(
        squares_kernel,
        out_shape=jax.ShapeDtypeStruct((1, query.shape[0] + key.shape[0]), jnp.float32),
        compiler_params=pltpu.CompilerParams(vmem_limit_bytes=VMEM_BYTES),
        name="squares",
    )(query, key)


def norm_keys_kernel(totals, key, value, gain, held):
    first = totals.shape[1] - key.shape[0]
    scale = as_columns(inverse_rms(totals[:, first:]))
    for start in range(0, key.shape[1], HS):
        lanes = slice(start, start + HS)
        held[0, :, lanes] = (key[:, lanes].astype(jnp.float32) * scale * gain[lanes][None]).astype(
            jnp.bfloat16
        )
    held[1] = value[...]


def norm_keys(totals, key, value, gain):
    return pl.pallas_call(
        norm_keys_kernel,
        out_shape=jax.ShapeDtypeStruct((2, *key.shape), jnp.bfloat16),
        compiler_params=pltpu.CompilerParams(vmem_limit_bytes=VMEM_BYTES),
        name="norm_keys",
    )(totals, key, value, gain)


def attention_kernel(
    lists, places, totals, query, cot, gain, key_gain, held, halo_n, halo_a,
    attended, grad_query, inner, gains, near, across_k, across_v, own_k, own_v,
    scale_cols, inner_sum, probs_low, grad_low,
):
    head = pl.program_id(0)
    rows = query.shape[0]
    span = held.shape[1]

    @pl.when(head == 0)
    def _():
        scale_cols[...] = as_columns(inverse_rms(totals[:, :rows]))
        inner_sum[...] = jnp.zeros_like(inner_sum)

    def closed(block, place):
        found = lists[block, 0] == place
        for entry in range(1, lists.shape[1]):
            found = jnp.logical_or(found, lists[block, entry] == place)
        return jnp.where(found, 0.0, EXCLUDED)

    def soften(lanes, slot, keys, values, normed, upstream, blocks):
        part = slice(blocks[0] * BLOCK, (blocks[-1] + 1) * BLOCK)
        scores = by_last(keys, normed[part])
        scores = jnp.concatenate(
            [scores[:span] + shut(blocks, 0), scores[span : 2 * span], scores[2 * span :] + shut(blocks, 1)],
            axis=0,
        )
        highest = jnp.max(scores, axis=0, keepdims=True)
        weights = jnp.exp2((scores - highest) * (FACTOR * LOG2E))
        share = 1.0 / jnp.sum(weights, axis=0, keepdims=True)
        probs_low[slot, :, part] = (weights * share).astype(jnp.bfloat16)
        grad_probs = by_last(values, upstream[part])
        delta = jnp.sum(weights * grad_probs, axis=0, keepdims=True) * share
        grad_low[slot, :, part] = (weights * ((grad_probs - delta) * (share * FACTOR))).astype(
            jnp.bfloat16
        )

    def shut(blocks, side):
        if len(blocks) == 1:
            return closed(blocks[0], places[side])
        return jnp.concatenate([jnp.full((1, BLOCK), closed(b, places[side])) for b in blocks], axis=1)

    def prepare(slot):
        lanes = slice(slot * HS, (slot + 1) * HS)
        raw = query[:, lanes].astype(jnp.float32)
        scaled = raw * scale_cols[...]
        normed = (scaled * gain[:, lanes]).astype(jnp.bfloat16)
        keys = jnp.concatenate([halo_n[0, :, lanes], held[0, :, lanes], halo_a[0, :, lanes]], axis=0)
        values = jnp.concatenate([halo_n[1, :, lanes], held[1, :, lanes], halo_a[1, :, lanes]], axis=0)
        return lanes, raw, scaled, normed, values, keys, cot[:, lanes]

    def finish(slot, lanes, raw, scaled, normed, values, keys, upstream):
        low = probs_low[slot]
        grads = grad_low[slot]
        attended[:, lanes] = plain(values.T, low).T.astype(jnp.bfloat16)
        grad = plain(keys.T, grads).T
        grad_query[:, lanes] = grad
        inner_sum[...] += raw * grad * gain[:, lanes]
        grad_keys = plain(grads, normed)
        grad_values = plain(low, upstream)
        gains[0:1, lanes] = jnp.sum(grad * scaled, axis=0, keepdims=True)
        gains[1:2, lanes] = (
            jnp.sum(grad_keys * keys.astype(jnp.float32), axis=0, keepdims=True)
            / key_gain[:, lanes]
        )
        near[0, :, lanes] = grad_keys[:span].astype(jnp.bfloat16)
        near[1, :, lanes] = grad_values[:span].astype(jnp.bfloat16)
        own_k[:, lanes] = grad_keys[span : 2 * span]
        own_v[:, lanes] = grad_values[span : 2 * span]
        across_k[:, lanes] = grad_keys[2 * span :].astype(jnp.bfloat16)
        across_v[:, lanes] = grad_values[2 * span :].astype(jnp.bfloat16)

    total = rows // BLOCK
    groups = [list(range(i, min(i + 2, total))) for i in range(0, total, 2)]
    ready = [prepare(slot) for slot in range(2)]
    for slot in range(2):
        lanes, raw, scaled, normed, values, keys, upstream = ready[slot]
        for blocks in groups:
            soften(lanes, slot, keys, values, normed, upstream, blocks)
        if slot and 1 == 1:
            finish(slot - 1, *ready[slot - 1])
        if 1 == 0:
            finish(slot, *ready[slot])
    if 1 == 1:
        finish(2 - 1, *ready[-1])

    @pl.when(head == pl.num_programs(0) - 1)
    def _():
        inner[...] = across_rows(inner_sum[...])


def attention(lists, places, totals, query, cot, gain, key_gain, held, halo_n, halo_a):
    rows, width = query.shape
    heads = width // (2 * HS)
    span = held.shape[1]

    def whole(shape):
        return pl.BlockSpec(shape, lambda h: (0,) * len(shape))

    def of_head(*lead):
        return pl.BlockSpec((*lead, 2 * HS), lambda h: (0,) * len(lead) + (h,))

    f32, bf16 = jnp.float32, jnp.bfloat16
    shape = jax.ShapeDtypeStruct
    scalars = pl.BlockSpec(memory_space=pltpu.SMEM)
    return pl.pallas_call(
        attention_kernel,
        grid=(heads,),
        in_specs=[scalars] * 2
        + [whole(totals.shape)]
        + [of_head(rows)] * 2
        + [of_head(1)] * 2
        + [of_head(2, span)] * 3,
        out_specs=[
            of_head(rows),
            of_head(rows),
            whole((1, rows)),
            of_head(2),
            of_head(2, span),
            of_head(span),
            of_head(span),
            of_head(span),
            of_head(span),
        ],
        out_shape=[
            shape((rows, width), bf16),
            shape((rows, width), f32),
            pltpu.HBM((1, rows), f32),
            pltpu.HBM((2, width), f32),
            pltpu.HBM((2, span, width), bf16),
            pltpu.HBM((span, width), bf16),
            pltpu.HBM((span, width), bf16),
            shape((span, width), f32),
            shape((span, width), f32),
        ],
        scratch_shapes=[
            pltpu.VMEM((rows, HS), f32),
            pltpu.VMEM((rows, HS), f32),
            pltpu.VMEM((2, 3 * span, rows), bf16),
            pltpu.VMEM((2, 3 * span, rows), bf16),
        ],
        compiler_params=pltpu.CompilerParams(vmem_limit_bytes=VMEM_BYTES),
        cost_estimate=pl.CostEstimate(
            flops=12 * rows * 3 * span * width, bytes_accessed=10 * rows * width, transcendentals=0
        ),
        name="attention",
    )(lists, places, totals, query, cot, gain, key_gain, held, halo_n, halo_a)


def combine_kernel(own, from_near, from_across, key, key_gain, inner_query, grad_key, inner):
    total = own[...] + from_near[0].astype(jnp.float32) + from_across[...].astype(jnp.float32)
    grad_key[...] = total
    rows = inner_query.shape[1]
    inner[:, :rows] = inner_query[...]
    inner[:, rows:] = across_rows(key[...].astype(jnp.float32) * (total * key_gain[...]))


def combine(own, from_near, from_across, key, key_gain, inner_query):
    shape = jax.ShapeDtypeStruct
    rows, width = own.shape
    whole = pl.BlockSpec(memory_space=pltpu.VMEM)
    first = pl.BlockSpec((1, rows, width), lambda i: (0, 0, 0))
    return pl.pallas_call(
        combine_kernel,
        grid=(1,),
        in_specs=[whole, first] + [whole] * 4,
        out_specs=[whole, whole],
        out_shape=[
            shape((rows, width), jnp.float32),
            shape((1, inner_query.shape[1] + rows), jnp.float32),
        ],
        compiler_params=pltpu.CompilerParams(vmem_limit_bytes=VMEM_BYTES),
        name="combine",
    )(own, from_near, from_across, key, key_gain, inner_query)


def norms_backward_kernel(
    totals, inner_parts, gains, query, grad_query, query_gain, key, grad_key, key_gain,
    own, from_near, from_across,
    query_out, key_out, value_out, query_gain_grad, key_gain_grad,
):
    rows = query.shape[0]
    inner = inner_parts[0]
    for index in range(1, len(inner_parts)):
        inner = inner + inner_parts[index]
    scale = inverse_rms(totals[...])
    shrink = scale * scale * scale * inner * (1.0 / D)

    def one(start, out, raw, grad, gain):
        here = slice(start, start + BLOCK)
        wide, less = as_columns(scale[:, here]), as_columns(shrink[:, here])
        first = start % rows
        there = slice(first, first + BLOCK)
        for lane in range(0, raw.shape[1], HS):
            lanes = slice(lane, lane + HS)
            out[there, lanes] = (
                wide * (grad[there, lanes] * gain[:, lanes])
                - raw[there, lanes].astype(jnp.float32) * less
            ).astype(jnp.bfloat16)

    for start in range(0, rows, BLOCK):
        one(start, query_out, query, grad_query, query_gain)
    one(rows, key_out, key, grad_key, key_gain)
    value_out[...] = (
        own[...] + from_near[0].astype(jnp.float32) + from_across[...].astype(jnp.float32)
    ).astype(jnp.bfloat16)
    query_gain_grad[...] = gains[0]
    key_gain_grad[...] = gains[1]


def norms_backward(totals, inner_parts, gains, *rest):
    query, key = rest[0], rest[3]
    count = len(inner_parts)

    def kernel(totals, *refs):
        parts = [ref[...] for ref in refs[:count]]
        norms_backward_kernel(totals, parts, *refs[count:])

    shape = jax.ShapeDtypeStruct
    width = query.shape[1]
    whole = pl.BlockSpec(memory_space=pltpu.VMEM)
    second = pl.BlockSpec((1, *key.shape), lambda i: (1, 0, 0))
    return pl.pallas_call(
        kernel,
        grid=(1,),
        in_specs=[whole] * (count + 9) + [second, whole],
        out_specs=[whole] * 5,
        out_shape=[
            shape(query.shape, jnp.bfloat16),
            shape(key.shape, jnp.bfloat16),
            shape(key.shape, jnp.bfloat16),
            shape((width,), jnp.float32),
            shape((width,), jnp.float32),
        ],
        compiler_params=pltpu.CompilerParams(vmem_limit_bytes=VMEM_BYTES),
        name="norms_backward",
    )(totals, *inner_parts, gains, *rest)


def in_hbm(value):
    return pltpu.with_memory_space_constraint(value, pltpu.HBM)


def swap_near(value):
    return lax.ppermute(value, "core", [(0, 1), (1, 0)])


def swap_across(value):
    size = 1
    for axis in LINE:
        size *= lax.axis_size(axis)
    pairs = []
    for i in range(1, size - 1, 2):
        pairs += [(i, i + 1), (i + 1, i)]
    return lax.ppermute(value, LINE, pairs)


def on_device(video_query, audio_key, audio_value, cotangent, query_gain, key_gain, time_lists):
    place = lax.axis_index(LINE)
    core = lax.axis_index("core")
    video_query, audio_key, audio_value, cotangent = (
        in_hbm(argument)
        for argument in (video_query, audio_key, audio_value, cotangent)
    )
    places = jnp.stack([place + 1 - 2 * core, place - 1 + 2 * core]).astype(jnp.int32)
    totals = lax.psum(squares(video_query, audio_key), "tp")
    held = norm_keys(totals, audio_key, audio_value, in_hbm(key_gain))
    query_gain = query_gain[None]
    key_gain = key_gain[None]
    halo_a = in_hbm(swap_across(held))
    halo_n = in_hbm(swap_near(held))
    (
        attended, grad_query, inner_query, gains, to_near, to_across_k, to_across_v, own_k, own_v
    ) = attention(
        time_lists,
        places,
        totals,
        video_query,
        cotangent,
        query_gain,
        key_gain,
        held,
        halo_n,
        halo_a,
    )
    from_near = swap_near(to_near)
    for axis in ("core", "x"):
        gains = lax.psum(gains, axis)
    gains, to_across_k, to_across_v = lax.optimization_barrier(
        (gains, to_across_k, to_across_v)
    )
    from_across_k = swap_across(to_across_k)
    from_across_v = swap_across(to_across_v)
    gains = lax.psum(gains, "y")
    grad_key, inner = combine(
        own_k, from_near, in_hbm(from_across_k), audio_key, key_gain, in_hbm(inner_query)
    )
    inner, gains = lax.optimization_barrier((inner, gains))
    size = lax.axis_size("tp")
    inner_parts = [inner] + [
        lax.ppermute(inner, "tp", [(i, (i + by) % size) for i in range(size)])
        for by in range(1, size)
    ]
    gains = lax.psum(gains, "far")
    video_query_grad, audio_key_grad, audio_value_grad, query_gain_grad, key_gain_grad = (
        norms_backward(
            totals,
            inner_parts,
            gains,
            video_query,
            grad_query,
            query_gain,
            audio_key,
            grad_key,
            key_gain,
            own_v,
            from_near,
            from_across_v,
        )
    )
    return (
        attended,
        video_query_grad,
        audio_key_grad,
        audio_value_grad,
        query_gain_grad,
        key_gain_grad,
    )


def solution(mesh):
    far = 4
    video, audio, tp = (mesh.shape[name] for name in ("video", "audio", "tp"))
    fine = Mesh(
        np.asarray(mesh.devices).reshape(video // far, far, audio // 2, 2, tp), (*LINE, "tp")
    )
    tokens = P(LINE, "tp")
    per_feature = P("tp")
    return jax.shard_map(
        on_device,
        mesh=fine,
        in_specs=(tokens, tokens, tokens, tokens, per_feature, per_feature, P(LINE, None)),
        out_specs=(tokens, tokens, tokens, tokens, per_feature, per_feature),
        check_vma=False,
    )
```
